32 devices in a mesh: seq: 8 (over y, x, core), dp: 4 (over z).
Axes of the slice: x: 2, y: 2, z: 4, core: 2. Of those that a mesh axis runs over, the one named last changes fastest.
Arguments:
- q_raw: bfloat16 [4, 1024, 1024], P('dp', 'seq'), may hold values from -21 to 21
- k_raw: bfloat16 [4, 1024, 256], P('dp', 'seq'), may hold values from -21 to 21
- v_raw: bfloat16 [4, 1024, 256], P('dp', 'seq'), may hold values from -6 to 6
- q_gain: float32 [128], P('dp'), may hold values from 0.5 to 6
- k_gain: float32 [128], P('dp'), may hold values from 0.5 to 6
- key_blocks: int32 [8, 8, 6], P('seq'), may hold values from -1 to 7, as said below
- d_context: bfloat16 [4, 1024, 1024], P('dp', 'seq'), may hold values from -21 to 21
Outputs:
- q_raw_grad: bfloat16 [4, 1024, 1024], P('dp', 'seq')
- k_raw_grad: bfloat16 [4, 1024, 256], P('dp', 'seq')
- v_grad: bfloat16 [4, 1024, 256], P('dp', 'seq')
- q_gain_grad: float32 [128], P('dp')
- k_gain_grad: float32 [128], P('dp')
The draws below stay inside these ranges and needn't reach their ends.
Inputs may be any that keep to these rules, and one draw needn't show every extreme that they name: key_blocks[h, b, 0] = b; slots 1 and 2 hold b - 1 and b + 1, or -1 past the ends of the sequence; the next 1 slots hold blocks 0 to 0; the last 2 slots hold drawn blocks, which may repeat earlier slots.
All inputs are finite; a program needn't handle non-finite values.
Results may differ from the reference program's by a relative error of at most 0.017.
The reference program's roundings to bfloat16 on the way count: a program that leaves them out, or rounds other values in their place, can miss the bound.
Values may be sent and summed in bfloat16 or wider, within the bound.
A program may use at most 64 MiB of HBM per device.

```python
import math
import jax
import jax.numpy as jnp
from jax import lax

HD = 128
HEADS = 8
D = 1024
KVD = 256
BLK = 128
GLOB = 1
RAND = 2
SEQ = 1024
NB = 8
SEQS = 4


def keys_base(key):
    noise = jax.random.truncated_normal(jax.random.fold_in(key, 11), -5.0, 5.0, (SEQS, SEQ, KVD), jnp.float32)
    return noise


def draw_k_raw(key, part):
    return keys_base(key).astype(jnp.bfloat16)


def draw_q_raw(key, part):
    noise = jax.random.truncated_normal(jax.random.fold_in(key, 12), -5.0, 5.0, (SEQS, SEQ, D), jnp.float32)
    return noise.astype(jnp.bfloat16)


def gain_draw(key, salt):
    low_end = jnp.log(0.5)
    high_end = jnp.log(2.0)
    return jnp.exp(jax.random.uniform(jax.random.fold_in(key, salt), (HD,), jnp.float32, low_end, high_end))


def draw_q_gain(key, part):
    return gain_draw(key, 21)


def draw_k_gain(key, part):
    return gain_draw(key, 22)


def draw_key_blocks(key, part):
    block_ids = jnp.broadcast_to(jnp.arange(NB)[None, :, None], (HEADS, NB, 1))
    before = jnp.where(block_ids > 0, block_ids - 1, -1)
    after = jnp.where(block_ids < NB - 1, block_ids + 1, -1)
    global_ids = jnp.broadcast_to(jnp.arange(GLOB)[None, None, :], (HEADS, NB, GLOB))
    drawn = jax.random.randint(jax.random.fold_in(key, 41), (HEADS, NB, RAND), 0, NB)
    return jnp.concatenate([block_ids, before, after, global_ids, drawn], axis=-1).astype(jnp.int32)


def draw_d_context(key, part):
    noise = jax.random.truncated_normal(jax.random.fold_in(key, 31), -5.0, 5.0, (SEQS, SEQ, D), jnp.float32)
    along = (0.5 + 1.5 * jnp.arange(SEQ) / SEQ)[None, :, None]
    across = (0.5 + jnp.arange(SEQS) / SEQS)[:, None, None]
    return (noise * along * across).astype(jnp.bfloat16)


def steps_of(rng, extent, split, least, largest):
    level = 1.0
    for dim, parts in split:
        steps = jax.random.uniform(jax.random.fold_in(jax.random.fold_in(rng, 6), dim), (parts,), jnp.float32, least / len(split), largest / len(split))
        level = level * jnp.repeat(jnp.exp(steps), extent[dim] // parts).reshape((-1,) + (1,) * (len(extent) - 1 - dim))
    return level


def gaussian(own_key, dims, scale, bound, split=(), held_as=jnp.bfloat16):
    entries = scale * jax.random.normal(own_key, dims, jnp.float32)
    if split:
        entries = entries * steps_of(own_key, dims, split, -0.22, 0.18)
    return jnp.clip(entries, -bound, bound).astype(held_as)


def setup_inputs(seed: int = 0) -> dict:
    keys = jax.random.split(jax.random.key(seed), 8)
    return {
        "q_raw": draw_q_raw(jax.random.fold_in(keys[7], 71), 0),
        "k_raw": draw_k_raw(jax.random.fold_in(keys[7], 71), 0),
        "v_raw": gaussian(keys[2], (SEQS, SEQ, KVD), 1.0, 6.0, ((0, 4), (1, 8))),
        "q_gain": draw_q_gain(jax.random.fold_in(keys[7], 71), 0),
        "k_gain": draw_k_gain(jax.random.fold_in(keys[7], 71), 0),
        "key_blocks": draw_key_blocks(jax.random.fold_in(keys[7], 71), 0),
        "d_context": draw_d_context(jax.random.fold_in(keys[7], 71), 0),
    }


EPSILON = 1e-06

def slot_keep(pattern):
    slot_count = pattern.shape[-1]
    present = pattern >= 0
    same_block = pattern[:, :, None] == pattern[:, None, :]
    earlier = jnp.arange(slot_count)[None, :] < jnp.arange(slot_count)[:, None]
    repeated = jnp.any(same_block & earlier[None, :, :], axis=2)
    return present & jnp.logical_not(repeated)

def norm_rows(raw_rows, gain_vec):
    length_total = raw_rows.shape[0]
    width = gain_vec.shape[0]
    values = raw_rows.astype(jnp.float32).reshape(length_total, -1, width)
    inverse = lax.rsqrt(lax.optimization_barrier(jnp.mean(values * values, axis=-1, keepdims=True)) + EPSILON)
    normed = (values * inverse * gain_vec).astype(jnp.bfloat16).reshape(length_total, -1)
    return (normed, inverse)

def norm_back(raw_rows, inverse, gain_vec, d_normed):
    length_total = raw_rows.shape[0]
    width = gain_vec.shape[0]
    values = raw_rows.astype(jnp.float32).reshape(length_total, -1, width)
    upstream = d_normed.astype(jnp.float32).reshape(length_total, -1, width)
    scaled = gain_vec * upstream
    row_total = lax.optimization_barrier(jnp.sum(scaled * values, axis=-1, keepdims=True))
    d_raw = inverse * scaled - inverse * inverse * inverse * values * row_total / width
    gain_part = lax.optimization_barrier(jnp.sum(upstream * values * inverse, axis=(0, 1)))
    return (d_raw.astype(jnp.bfloat16).reshape(length_total, -1), gain_part)

def rounded(values):
    return lax.optimization_barrier(values.astype(jnp.bfloat16)).astype(jnp.float32)

def softmax_rows(score_matrix, axes):
    row_peak = lax.optimization_barrier(jnp.max(score_matrix, axis=axes, keepdims=True))
    raised = jnp.exp(score_matrix - row_peak)
    return raised / lax.optimization_barrier(jnp.sum(raised, axis=axes, keepdims=True))

def head_pass(q_head, k_head, v_head, d_head, pattern):
    length_total, width_per_head = q_head.shape
    blocks = length_total // BLK
    lead_rows = GLOB * BLK
    logit_scale = 1.0 / math.sqrt(width_per_head)
    keep_slot = slot_keep(pattern)
    picked = jnp.maximum(pattern, 0).astype(jnp.int32)
    top_precision = lax.Precision.HIGHEST
    query_tiles = q_head.astype(jnp.float32).reshape(blocks, BLK, width_per_head)
    k_tiles = k_head.astype(jnp.float32).reshape(blocks, BLK, width_per_head)
    v_tiles = v_head.astype(jnp.float32).reshape(blocks, BLK, width_per_head)
    tile_gradient = d_head.astype(jnp.float32).reshape(blocks, BLK, width_per_head)
    selected_keys = k_tiles[picked]
    selected_values = v_tiles[picked]
    score_matrix = jnp.einsum('vfy,vtwy->vftw', query_tiles, selected_keys, precision=top_precision) * logit_scale
    score_matrix = jnp.where(keep_slot[:, None, :, None], score_matrix, -jnp.inf)
    weights = softmax_rows(score_matrix, (2, 3))
    weight_reduced = rounded(weights)
    sparse_query_row = (jnp.arange(blocks) >= GLOB)[:, None, None, None]
    weight_gradient = jnp.einsum('vfy,vtwy->vftw', tile_gradient, selected_values, precision=top_precision)
    row_delta = lax.optimization_barrier(jnp.sum(weights * weight_gradient, axis=(2, 3), keepdims=True))
    score_gradient = rounded(jnp.where(sparse_query_row, weights * (weight_gradient - row_delta) * logit_scale, 0.0))
    query_sparse = jnp.einsum('lgnw,lnwi->lgi', score_gradient, selected_keys, precision=top_precision).reshape(length_total, width_per_head)
    key_pieces = jnp.einsum('otnc,otj->oncj', score_gradient, query_tiles, precision=top_precision)
    value_pieces = jnp.einsum('otnc,otj->oncj', jnp.where(sparse_query_row, weight_reduced, 0.0), tile_gradient, precision=top_precision)
    one_hot = ((picked[:, :, None] == jnp.arange(blocks)[None, None, :]) & keep_slot[:, :, None]).astype(jnp.float32)
    k_sparse = jnp.einsum('bsn,bskd->nkd', one_hot, key_pieces, precision=top_precision).reshape(length_total, width_per_head)
    v_sparse = jnp.einsum('bsn,bskd->nkd', one_hot, value_pieces, precision=top_precision).reshape(length_total, width_per_head)
    q_lead = q_head[:lead_rows]
    d_lead = d_head[:lead_rows]
    lead_scores = jnp.dot(q_lead, k_head.T, preferred_element_type=jnp.float32) * logit_scale
    lead_weights = softmax_rows(lead_scores, (1,))
    lead_low = lead_weights.astype(jnp.bfloat16)
    lead_dprob = jnp.dot(d_lead, v_head.T, preferred_element_type=jnp.float32)
    lead_delta = lax.optimization_barrier(jnp.sum(lead_weights * lead_dprob, axis=1, keepdims=True))
    lead_dscore = (lead_weights * (lead_dprob - lead_delta) * logit_scale).astype(jnp.bfloat16)
    lead_dq = jnp.dot(lead_dscore, k_head, preferred_element_type=jnp.float32)
    lead_dk = jnp.dot(lead_dscore.T, q_lead, preferred_element_type=jnp.float32)
    lead_dv = jnp.dot(lead_low.T, d_lead, preferred_element_type=jnp.float32)
    d_query = jnp.concatenate([lead_dq, query_sparse[lead_rows:]], axis=0).astype(jnp.bfloat16)
    return (d_query, k_sparse + lead_dk, v_sparse + lead_dv)

def reference(q_raw, k_raw, v_raw, q_gain, k_gain, key_blocks, d_context):
    head_count = key_blocks.shape[0]
    width_per_head = q_gain.shape[0]
    kv_count = k_raw.shape[2] // width_per_head
    group_len = head_count // kv_count

    def one_sequence(inputs):
        q_seq, k_seq, v_seq, d_seq = inputs
        length_total = q_seq.shape[0]
        q_normed, q_inverse = norm_rows(q_seq, q_gain)
        k_normed, k_inverse = norm_rows(k_seq, k_gain)

        def split_heads(block_array):
            return jnp.transpose(block_array.reshape(length_total, -1, width_per_head), (1, 0, 2))

        def widen(block_array):
            return jnp.repeat(split_heads(block_array), group_len, axis=0)

        def one_head(head_items):
            return head_pass(head_items[0], head_items[1], head_items[2], head_items[3], head_items[4])
        results = lax.map(one_head, (split_heads(q_normed), widen(k_normed), widen(v_seq), split_heads(d_seq), key_blocks))
        d_q_normed = jnp.transpose(results[0], (1, 0, 2)).reshape(length_total, head_count * width_per_head)

        def fold_group(head_terms):
            summed = lax.optimization_barrier(jnp.sum(head_terms.reshape(kv_count, group_len, length_total, width_per_head), axis=1)).astype(jnp.bfloat16)
            return jnp.transpose(summed, (1, 0, 2)).reshape(length_total, kv_count * width_per_head)
        d_k_normed = fold_group(results[1])
        v_grad = fold_group(results[2])
        q_grad, q_part = norm_back(q_seq, q_inverse, q_gain, d_q_normed)
        k_grad, k_part = norm_back(k_seq, k_inverse, k_gain, d_k_normed)
        return (q_grad, k_grad, v_grad, q_part, k_part)
    outputs = lax.map(one_sequence, (q_raw, k_raw, v_raw, d_context))
    return (outputs[0], outputs[1], outputs[2], lax.optimization_barrier(jnp.sum(outputs[3], axis=0)), lax.optimization_barrier(jnp.sum(outputs[4], axis=0)))
```

```python
import functools
import math

import jax
import jax.numpy as jnp
from jax import lax
from jax.experimental import pallas as pl
from jax.experimental.pallas import tpu as pltpu
from jax.sharding import PartitionSpec as P

BLK = 128
GLOB = 1


EPSILON = 1e-06


def slot_keep(pattern):
    slot_count = pattern.shape[-1]
    present = pattern >= 0
    same_block = pattern[:, :, None] == pattern[:, None, :]
    earlier = jnp.arange(slot_count)[None, :] < jnp.arange(slot_count)[:, None]
    repeated = jnp.any(same_block & earlier[None, :, :], axis=2)
    return present & jnp.logical_not(repeated)


def norm_rows(raw_rows, gain_vec):
    length_total = raw_rows.shape[0]
    width = gain_vec.shape[0]
    values = raw_rows.astype(jnp.float32).reshape(length_total, -1, width)
    inverse = lax.rsqrt(jnp.mean(values * values, axis=-1, keepdims=True) + EPSILON)
    normed = (values * inverse * gain_vec).astype(jnp.bfloat16).reshape(length_total, -1)
    return (normed, inverse)


def norm_back(raw_rows, inverse, gain_vec, d_normed):
    length_total = raw_rows.shape[0]
    width = gain_vec.shape[0]
    values = raw_rows.astype(jnp.float32).reshape(length_total, -1, width)
    upstream = d_normed.astype(jnp.float32).reshape(length_total, -1, width)
    scaled = gain_vec * upstream
    row_total = jnp.sum(scaled * values, axis=-1, keepdims=True)
    d_raw = inverse * scaled - inverse * inverse * inverse * values * row_total / width
    gain_part = jnp.sum(upstream * values * inverse, axis=(0, 1))
    return (d_raw.astype(jnp.bfloat16).reshape(length_total, -1), gain_part)


def softmax_rows(score_matrix, axes):
    row_peak = jnp.max(score_matrix, axis=axes, keepdims=True)
    raised = jnp.exp(score_matrix - row_peak)
    return raised / jnp.sum(raised, axis=axes, keepdims=True)


def tile_layout(head_array):
    length_total, width_per_head = head_array.shape
    return head_array.reshape(length_total // BLK, BLK, width_per_head)


def group_size(blocks):
    return math.gcd(blocks, max(1, 1024 // BLK))


def backward_head(q_head, k_head, v_head, d_head, pattern):
    length_total, width_per_head = q_head.shape
    blocks = length_total // BLK
    lead_rows = GLOB * BLK
    logit_scale = 1.0 / math.sqrt(width_per_head)
    keep_slot = slot_keep(pattern)
    picked = jnp.maximum(pattern, 0)
    query_tiles = tile_layout(q_head)
    k_tiles = tile_layout(k_head)
    v_tiles = tile_layout(v_head)
    tile_gradient = tile_layout(d_head)
    group_len = group_size(blocks)
    top_precision = lax.Precision.HIGHEST

    def one_group(carry, group_index):
        k_acc, v_acc = carry
        first_block = group_index * group_len
        query_rows = lax.dynamic_slice_in_dim(query_tiles, first_block, group_len, 0)
        grad_rows = lax.dynamic_slice_in_dim(tile_gradient, first_block, group_len, 0)
        chosen = lax.dynamic_slice_in_dim(picked, first_block, group_len, 0)
        allowed = lax.dynamic_slice_in_dim(keep_slot, first_block, group_len, 0)
        selected_keys = k_tiles[chosen]
        selected_values = v_tiles[chosen]
        score_matrix = (
            jnp.einsum(
                "gqd,gskd->gqsk", query_rows, selected_keys, preferred_element_type=jnp.float32
            )
            * logit_scale
        )
        score_matrix = jnp.where(allowed[:, None, :, None], score_matrix, -jnp.inf)
        weights = softmax_rows(score_matrix, (2, 3))
        weight_reduced = weights.astype(jnp.bfloat16)
        sparse_query_row = (first_block + jnp.arange(group_len) >= GLOB)[:, None, None, None]
        weight_gradient = jnp.einsum(
            "gqd,gskd->gqsk", grad_rows, selected_values, preferred_element_type=jnp.float32
        )
        row_delta = jnp.sum(weights * weight_gradient, axis=(2, 3), keepdims=True)
        score_gradient = jnp.where(
            sparse_query_row, weights * (weight_gradient - row_delta) * logit_scale, 0.0
        ).astype(jnp.bfloat16)
        d_query = jnp.einsum(
            "gqsk,gskd->gqd", score_gradient, selected_keys, preferred_element_type=jnp.float32
        )
        key_pieces = jnp.einsum(
            "gqsk,gqd->gskd", score_gradient, query_rows, preferred_element_type=jnp.float32
        )
        kept_low = jnp.where(sparse_query_row, weight_reduced, jnp.zeros_like(weight_reduced))
        value_pieces = jnp.einsum(
            "gqsk,gqd->gskd", kept_low, grad_rows, preferred_element_type=jnp.float32
        )
        one_hot = (
            (chosen[:, :, None] == jnp.arange(blocks)[None, None, :]) & allowed[:, :, None]
        ).astype(jnp.float32)
        k_acc = k_acc + jnp.einsum("gsn,gskd->nkd", one_hot, key_pieces, precision=top_precision)
        v_acc = v_acc + jnp.einsum("gsn,gskd->nkd", one_hot, value_pieces, precision=top_precision)
        return ((k_acc, v_acc), d_query)

    zero_acc = jnp.zeros((blocks, BLK, width_per_head), jnp.float32)
    sums, q_groups = lax.scan(one_group, (zero_acc, zero_acc), jnp.arange(blocks // group_len))
    query_sparse = q_groups.reshape(length_total, width_per_head)
    k_sparse = sums[0].reshape(length_total, width_per_head)
    v_sparse = sums[1].reshape(length_total, width_per_head)
    q_lead = q_head[:lead_rows]
    d_lead = d_head[:lead_rows]
    lead_scores = (
        jnp.einsum("qd,kd->qk", q_lead, k_head, preferred_element_type=jnp.float32) * logit_scale
    )
    lead_weights = softmax_rows(lead_scores, (1,))
    lead_low = lead_weights.astype(jnp.bfloat16)
    lead_dprob = jnp.einsum("qd,kd->qk", d_lead, v_head, preferred_element_type=jnp.float32)
    lead_delta = jnp.sum(lead_weights * lead_dprob, axis=1, keepdims=True)
    lead_dscore = (lead_weights * (lead_dprob - lead_delta) * logit_scale).astype(jnp.bfloat16)
    lead_dq = jnp.dot(lead_dscore, k_head, preferred_element_type=jnp.float32)
    lead_dk = jnp.einsum("qk,qd->kd", lead_dscore, q_lead, preferred_element_type=jnp.float32)
    lead_dv = jnp.einsum("qk,qd->kd", lead_low, d_lead, preferred_element_type=jnp.float32)
    d_query = jnp.concatenate([lead_dq, query_sparse[lead_rows:]], axis=0).astype(jnp.bfloat16)
    return (d_query, k_sparse + lead_dk, v_sparse + lead_dv)


def widen_heads(rows, width_per_head, group_len):
    tokens = rows.shape[0]
    kv_count = rows.shape[1] // width_per_head
    spread = jnp.broadcast_to(
        rows.reshape(tokens, kv_count, 1, width_per_head),
        (tokens, kv_count, group_len, width_per_head),
    )
    return spread.reshape(tokens, kv_count * group_len * width_per_head)


def shards_by_head(q_raw, k_raw, v_raw, q_gain, k_gain, key_blocks, d_context):
    q_full, k_full = (
        lax.all_gather(q_gain, "dp", axis=0, tiled=True),
        lax.all_gather(k_gain, "dp", axis=0, tiled=True),
    )
    q_normed, q_inverse = norm_rows(q_raw[0], q_full)
    k_normed, k_inverse = norm_rows(k_raw[0], k_full)
    width_per_head = q_full.shape[0]
    group_len = q_raw.shape[2] // k_raw.shape[2]
    tokens = q_raw.shape[1]
    k_wide = widen_heads(k_normed, width_per_head, group_len)
    v_wide = widen_heads(v_raw[0], width_per_head, group_len)
    q_heads, k_heads, v_heads, d_heads = (
        lax.all_to_all(q_normed, "seq", split_axis=1, concat_axis=0, tiled=True),
        lax.all_to_all(k_wide, "seq", split_axis=1, concat_axis=0, tiled=True),
        lax.all_to_all(v_wide, "seq", split_axis=1, concat_axis=0, tiled=True),
        lax.all_to_all(d_context[0], "seq", split_axis=1, concat_axis=0, tiled=True),
    )
    length_total = q_heads.shape[0]
    head_count = key_blocks.shape[0]

    def split_heads(head_array):
        return head_array.reshape(length_total, head_count, width_per_head)

    def merge_heads(head_array):
        return head_array.reshape(length_total, head_count * width_per_head)

    backward = jax.vmap(backward_head, in_axes=(1, 1, 1, 1, 0), out_axes=1)
    dq_heads, dk_heads, dv_heads = backward(
        split_heads(q_heads),
        split_heads(k_heads),
        split_heads(v_heads),
        split_heads(d_heads),
        key_blocks,
    )
    dq_heads = merge_heads(dq_heads)
    dk_heads = merge_heads(dk_heads)
    dv_heads = merge_heads(dv_heads)
    d_q_normed = lax.all_to_all(dq_heads, "seq", split_axis=0, concat_axis=1, tiled=True)
    dk_terms, dv_terms = (
        lax.all_to_all(dk_heads, "seq", split_axis=0, concat_axis=1, tiled=True),
        lax.all_to_all(dv_heads, "seq", split_axis=0, concat_axis=1, tiled=True),
    )
    kv_count = k_raw.shape[2] // width_per_head
    d_k_normed = (
        jnp.sum(dk_terms.reshape(tokens, kv_count, group_len, width_per_head), axis=2)
        .astype(jnp.bfloat16)
        .reshape(tokens, kv_count * width_per_head)
    )
    v_grad = (
        jnp.sum(dv_terms.reshape(tokens, kv_count, group_len, width_per_head), axis=2)
        .astype(jnp.bfloat16)
        .reshape(tokens, kv_count * width_per_head)
    )
    q_grad, q_part = norm_back(q_raw[0], q_inverse, q_full, d_q_normed)
    k_grad, k_part = norm_back(k_raw[0], k_inverse, k_full, d_k_normed)
    q_total, k_total = lax.psum((q_part, k_part), ("seq", "dp"))
    shard_len = q_gain.shape[0]
    offset = lax.axis_index("dp") * shard_len
    q_gain_grad = lax.dynamic_slice_in_dim(q_total, offset, shard_len)
    k_gain_grad = lax.dynamic_slice_in_dim(k_total, offset, shard_len)
    return (q_grad[None], k_grad[None], v_grad[None], q_gain_grad, k_gain_grad)


F32 = jnp.float32
BF16 = jnp.bfloat16
MESH = pl.DeviceIdType.MESH
VMEM_ROOM = 56 * 1024 * 1024


def token_kernel(
    n, dpn,
    q_in, k_in, v_in, gq_in, gk_in, kb_in, d_in,
    q_out, k_out, v_out, gq_out, gk_out,
    q_s, d_s, k_all, v_all, kb_all, kbm, gq_all, gk_all, bias,
    q_hat, q_inv, q_st, q_tr, d_st, d_tr, k_hat, k_tr,
    s_scr, p_scr, ds_scr, acc, sib_out, sib_in, chip_out, chip_in,
    q_res, part1, part2,
    loc, k_snd, k_rcv, v_snd, v_rcv, kf_snd, kf_rcv, vf_snd, vf_rcv,
    b_snd, b_rcv, gq_snd, gq_rcv, gk_snd, gk_rcv,
    s_snd, s_rcv, x_snd, x_rcv, p1_snd, p1_rcv, p2_snd, p2_rcv,
):
    nc = n // 2
    hd = q_hat.shape[2]
    tokens = q_s.shape[0]
    heads = q_s.shape[1] // hd
    groups = k_in.shape[1] // hd
    per = heads // groups
    wide = per * tokens
    scale = 1.0 / math.sqrt(hd)
    raise_by = scale * math.log2(math.e)

    me = lax.axis_index("seq")
    md = lax.axis_index("dp")
    core = lax.rem(me, 2)
    chip = lax.div(me, 2)
    sib = 2 * chip + 1 - core

    def src_chip(t):
        return lax.rem(chip + nc - t, nc)

    def dst_chip(t):
        return lax.rem(chip + t, nc)

    def send(src, dst, snd, rcv, **where):
        return pltpu.make_async_remote_copy(
            src_ref=src, dst_ref=dst, send_sem=snd, recv_sem=rcv,
            device_id=where, device_id_type=MESH,
        )

    def local(src, dst, i):
        copy = pltpu.make_async_copy(src, dst, loc.at[i])
        copy.start()
        return copy

    own_k = local(k_in, k_all.at[me], 0)
    own_v = local(v_in, v_all.at[me], 1)
    own_gq = local(gq_in, gq_all.at[md], 2)
    own_gk = local(gk_in, gk_all.at[md], 3)
    own_kb = local(kb_in, kb_all.at[me], 4)
    own_q = local(q_in, q_s, 5)
    own_d = local(d_in, d_s, 6)

    barrier = pltpu.get_barrier_semaphore()
    for r in range(1, n):
        pl.semaphore_signal(barrier, inc=1, device_id={"seq": lax.rem(me + r, n)}, device_id_type=MESH)
    for r in range(1, dpn):
        pl.semaphore_signal(barrier, inc=1, device_id={"dp": lax.rem(md + r, dpn)}, device_id_type=MESH)
    pl.semaphore_wait(barrier, n - 1 + dpn - 1)

    pending = []

    def go(copy):
        copy.start()
        pending.append(copy)

    for r in range(1, dpn):
        to = lax.rem(md + r, dpn)
        go(send(gq_in, gq_all.at[md], gq_snd.at[r], gq_rcv.at[r], dp=to))
        go(send(gk_in, gk_all.at[md], gk_snd.at[r], gk_rcv.at[r], dp=to))
    for t in range(1, nc):
        go(send(k_in, k_all.at[me], k_snd.at[t], k_rcv.at[t], seq=2 * dst_chip(t) + core))
    go(send(k_in, k_all.at[me], k_snd.at[0], k_rcv.at[0], seq=sib))
    for t in range(1, nc):
        go(send(v_in, v_all.at[me], v_snd.at[t], v_rcv.at[t], seq=2 * dst_chip(t) + core))
    go(send(v_in, v_all.at[me], v_snd.at[0], v_rcv.at[0], seq=sib))
    for r in range(1, n):
        go(send(kb_in, kb_all.at[me], b_snd.at[r], b_rcv.at[r], seq=lax.rem(me + r, n)))

    def arrived(ref, snd, rcv):
        send(ref, ref, snd, rcv, seq=sib).wait_recv()

    own_d.wait()
    for h in range(heads):
        g, i = h // per, h % per
        rows = slice(i * tokens, (i + 1) * tokens)
        x = d_s[:, h * hd:(h + 1) * hd]
        d_st[g, rows, :] = x
        d_tr[g, :, rows] = x.astype(F32).T.astype(BF16)
    own_q.wait()
    own_gq.wait()
    own_gk.wait()
    for r in range(1, dpn):
        frm = lax.rem(md + dpn - r, dpn)
        arrived(gq_all.at[frm], gq_snd.at[r], gq_rcv.at[r])
        arrived(gk_all.at[frm], gk_snd.at[r], gk_rcv.at[r])
    q_gain = jnp.concatenate([gq_all[i] for i in range(dpn)], axis=1)
    k_gain = jnp.concatenate([gk_all[i] for i in range(dpn)], axis=1)
    for h in range(heads):
        g, i = h // per, h % per
        rows = slice(i * tokens, (i + 1) * tokens)
        x = q_s[:, h * hd:(h + 1) * hd].astype(F32)
        inv = lax.rsqrt(jnp.mean(x * x, axis=1, keepdims=True) + EPSILON)
        inv = jnp.broadcast_to(inv, (tokens, hd))
        x = x * inv
        q_inv[h] = inv
        q_hat[h] = x
        x = x * q_gain
        q_st[g, rows, :] = x.astype(BF16)
        q_tr[g, :, rows] = x.T.astype(BF16)

    own_kb.wait()
    for r in range(1, n):
        arrived(kb_all.at[lax.rem(me + n - r, n)], b_snd.at[r], b_rcv.at[r])
    held = kb_all.shape[1]
    for h in range(heads):
        kbm[h:h + 1, :] = kb_all[h // held, h % held, pl.ds(me, 1), :]
    named = kbm[...]
    for j in range(n):
        hit = jnp.where((named == j) | (me < GLOB), 0.0, -jnp.inf)
        bias[j] = jnp.broadcast_to(jnp.max(hit, axis=1, keepdims=True), (heads, tokens))

    def forward(t):
        frm = 2 * src_chip(t) + core
        arrived(k_all.at[frm], k_snd.at[t], k_rcv.at[t])
        go(send(k_all.at[frm], k_all.at[frm], kf_snd.at[t], kf_rcv.at[t], seq=sib))
        arrived(v_all.at[frm], v_snd.at[t], v_rcv.at[t])
        go(send(v_all.at[frm], v_all.at[frm], vf_snd.at[t], vf_rcv.at[t], seq=sib))

    peak = [jnp.full((1, wide), -jnp.inf, F32) for _ in range(groups)]

    def pair(t):
        at = src_chip(t)
        if t == 0:
            own_k.wait()
            arrived(k_all.at[sib], k_snd.at[0], k_rcv.at[0])
        else:
            arrived(k_all.at[2 * at + 1 - core], kf_snd.at[t], kf_rcv.at[t])
        keys = k_all[pl.ds(2 * at, 2)].reshape(2 * tokens, groups * hd)
        for g in range(groups):
            x = keys[:, g * hd:(g + 1) * hd].astype(F32)
            inv = lax.rsqrt(jnp.mean(x * x, axis=1, keepdims=True) + EPSILON)
            x = x * inv
            k_hat[t, g] = x
            x = x * k_gain
            k_tr[t, g] = x.T.astype(BF16)
            s = jnp.dot(x.astype(BF16), q_tr[g], preferred_element_type=F32)
            for i in range(2):
                block = bias[2 * at + i]
                line = jnp.concatenate([block[h:h + 1] for h in range(g * per, (g + 1) * per)], axis=1)
                part = s[i * tokens:(i + 1) * tokens] + line
                s_scr[t, g, i * tokens:(i + 1) * tokens, :] = part
                peak[g] = jnp.maximum(peak[g], jnp.max(part, axis=0, keepdims=True))
        if t == 0:
            own_v.wait()
            arrived(v_all.at[sib], v_snd.at[0], v_rcv.at[0])
        else:
            arrived(v_all.at[2 * at + 1 - core], vf_snd.at[t], vf_rcv.at[t])
        vals = v_all[pl.ds(2 * at, 2)].reshape(2 * tokens, groups * hd)
        for g in range(groups):
            p_scr[t, g] = jnp.dot(vals[:, g * hd:(g + 1) * hd], d_tr[g], preferred_element_type=F32)

    for t in range(nc):
        if t + 1 < nc:
            forward(t + 1)
        pair(t)

    norm, delta = [], []
    for g in range(groups):
        total = jnp.zeros((1, wide), F32)
        cross = jnp.zeros((1, wide), F32)
        for t in range(nc):
            e = jnp.exp2((s_scr[t, g] - peak[g]) * raise_by)
            s_scr[t, g] = e
            total = total + jnp.sum(e, axis=0, keepdims=True)
            cross = cross + jnp.sum(e * p_scr[t, g], axis=0, keepdims=True)
        inv = 1.0 / total
        norm.append(inv)
        delta.append(cross * inv)

    k_part = jnp.zeros((1, hd), F32)

    def hand_on(t):
        arrived(sib_in.at[t], s_snd.at[t], s_rcv.at[t])
        chip_out[t] = (acc[t, core] + sib_in[t].astype(F32)).astype(BF16)
        go(send(chip_out.at[t], chip_in.at[t], x_snd.at[t], x_rcv.at[t], seq=2 * src_chip(t) + core))

    order = list(range(1, nc)) + [0]
    for pos, t in enumerate(order):
        for g in range(groups):
            w = s_scr[t, g] * norm[g]
            ds = (w * (p_scr[t, g] - delta[g]) * scale).astype(BF16)
            ds_scr[t, g] = ds
            dk = jnp.dot(ds, q_st[g], preferred_element_type=F32)
            dv = jnp.dot(w.astype(BF16), d_st[g], preferred_element_type=F32)
            cols = slice(g * hd, (g + 1) * hd)
            for i in range(2):
                acc[t, i, 0, :, cols] = dk[i * tokens:(i + 1) * tokens]
                acc[t, i, 1, :, cols] = dv[i * tokens:(i + 1) * tokens]
            k_part = k_part + jnp.sum(dk * k_hat[t, g], axis=0, keepdims=True)
        sib_out[t] = acc[t, 1 - core].astype(BF16)
        go(send(sib_out.at[t], sib_in.at[t], s_snd.at[t], s_rcv.at[t], seq=sib))
        if pos >= 1:
            hand_on(order[pos - 1])

    q_part = jnp.zeros((1, hd), F32)
    for g in range(groups):
        dq_tr = jnp.zeros((hd, wide), F32)
        for t in range(nc):
            dq_tr = dq_tr + jnp.dot(k_tr[t, g], ds_scr[t, g], preferred_element_type=F32)
        for i in range(per):
            h = g * per + i
            dq = dq_tr[:, i * tokens:(i + 1) * tokens].T.astype(BF16).astype(F32)
            x = q_hat[h]
            q_part = q_part + jnp.sum(dq * x, axis=0, keepdims=True)
            y = dq * q_gain
            mean = jnp.mean(y * x, axis=1, keepdims=True)
            q_res[:, h * hd:(h + 1) * hd] = (q_inv[h] * (y - x * mean)).astype(BF16)
    out_q = local(q_res, q_out, 5)

    part1[md] = jnp.concatenate([q_part, k_part, jnp.zeros((6, hd), F32)], axis=0)
    for r in range(1, dpn):
        go(send(part1.at[md], part1.at[md], p1_snd.at[r], p1_rcv.at[r], dp=lax.rem(md + r, dpn)))
    arrived(sib_in.at[0], s_snd.at[0], s_rcv.at[0])
    total = acc[0, core] + sib_in[0].astype(F32)
    for r in range(1, dpn):
        arrived(part1.at[lax.rem(md + dpn - r, dpn)], p1_snd.at[r], p1_rcv.at[r])
    gains = part1[0]
    for i in range(1, dpn):
        gains = gains + part1[i]
    part2[me] = gains
    for r in range(1, n):
        go(send(part2.at[me], part2.at[me], p2_snd.at[r], p2_rcv.at[r], seq=lax.rem(me + r, n)))

    for t in range(1, nc):
        arrived(chip_in.at[t], x_snd.at[t], x_rcv.at[t])
        total = total + chip_in[t].astype(F32)
    v_out[...] = total[1].astype(BF16)
    dk_all = total[0].astype(BF16).astype(F32)
    for g in range(groups):
        cols = slice(g * hd, (g + 1) * hd)
        x = k_all[me, :, cols].astype(F32)
        inv = lax.rsqrt(jnp.mean(x * x, axis=1, keepdims=True) + EPSILON)
        x = x * inv
        y = dk_all[:, cols] * k_gain
        mean = jnp.mean(y * x, axis=1, keepdims=True)
        k_out[:, cols] = (inv * (y - x * mean)).astype(BF16)

    for r in range(1, n):
        arrived(part2.at[lax.rem(me + n - r, n)], p2_snd.at[r], p2_rcv.at[r])
    gains = part2[0]
    for i in range(1, n):
        gains = gains + part2[i]
    share = hd // dpn
    mine = jnp.zeros((8, share), F32)
    for i in range(dpn):
        mine = mine + jnp.where(md == i, gains[:, i * share:(i + 1) * share], 0.0)
    gq_out[...] = mine[0:1]
    gk_out[...] = mine[1:2]

    out_q.wait()
    for copy in pending:
        copy.wait_send()


def scratch_list(n, dpn, tokens, hd, heads, groups, held, blocks, slots):
    nc = n // 2
    wide = heads // groups * tokens
    vm = pltpu.VMEM
    dma = pltpu.SemaphoreType.DMA
    kvd = groups * hd
    arrays = [
        vm((tokens, heads * hd), BF16),
        vm((tokens, heads * hd), BF16),
        vm((n, tokens, kvd), BF16),
        vm((n, tokens, kvd), BF16),
        vm((n, held, blocks, slots), jnp.int32),
        vm((heads, slots), jnp.int32),
        vm((dpn, 1, hd // dpn), F32),
        vm((dpn, 1, hd // dpn), F32),
        vm((n, heads, tokens), F32),
        vm((heads, tokens, hd), F32),
        vm((heads, tokens, hd), F32),
        vm((groups, wide, hd), BF16),
        vm((groups, hd, wide), BF16),
        vm((groups, wide, hd), BF16),
        vm((groups, hd, wide), BF16),
        vm((nc, groups, 2 * tokens, hd), F32),
        vm((nc, groups, hd, 2 * tokens), BF16),
        vm((nc, groups, 2 * tokens, wide), F32),
        vm((nc, groups, 2 * tokens, wide), F32),
        vm((nc, groups, 2 * tokens, wide), BF16),
        vm((nc, 2, 2, tokens, kvd), F32),
        vm((nc, 2, tokens, kvd), BF16),
        vm((nc, 2, tokens, kvd), BF16),
        vm((nc, 2, tokens, kvd), BF16),
        vm((nc, 2, tokens, kvd), BF16),
        vm((tokens, heads * hd), BF16),
        vm((dpn, 8, hd), F32),
        vm((n, 8, hd), F32),
    ]
    sems = [dma((7,))] + [dma((nc,))] * 8 + [dma((n,))] * 2 + [dma((dpn,))] * 4
    sems += [dma((nc,))] * 4 + [dma((dpn,))] * 2 + [dma((n,))] * 2
    return arrays, sems


def shards(n, dpn, q_raw, k_raw, v_raw, q_gain, k_gain, key_blocks, d_context):
    hd = q_gain.shape[0] * dpn
    tokens = q_raw.shape[1]
    heads = q_raw.shape[2] // hd
    groups = k_raw.shape[2] // hd
    held, blocks, slots = key_blocks.shape
    arrays, sems = scratch_list(n, dpn, tokens, hd, heads, groups, held, blocks, slots)
    room = sum(math.prod(a.shape) * jnp.dtype(a.dtype).itemsize for a in arrays)
    fits = room < VMEM_ROOM - 16 * 1024 * 1024
    if n % 2 or tokens != BLK or q_raw.shape[0] != 1 or not fits:
        return shards_by_head(q_raw, k_raw, v_raw, q_gain, k_gain, key_blocks, d_context)
    anywhere = pl.BlockSpec(memory_space=pl.ANY)
    vmem = pl.BlockSpec(memory_space=pltpu.VMEM)
    share = hd // dpn
    kvd = groups * hd
    q_grad, k_grad, v_grad, gq, gk = pl.pallas_call(
        functools.partial(token_kernel, n, dpn),
        out_shape=(
            jax.ShapeDtypeStruct((tokens, heads * hd), BF16),
            jax.ShapeDtypeStruct((tokens, kvd), BF16),
            jax.ShapeDtypeStruct((tokens, kvd), BF16),
            jax.ShapeDtypeStruct((1, share), F32),
            jax.ShapeDtypeStruct((1, share), F32),
        ),
        in_specs=[anywhere] * 7,
        out_specs=(anywhere, vmem, vmem, vmem, vmem),
        scratch_shapes=arrays + sems,
        compiler_params=pltpu.CompilerParams(
            collective_id=0, has_side_effects=True, vmem_limit_bytes=VMEM_ROOM
        ),
    )(q_raw[0], k_raw[0], v_raw[0], q_gain[None], k_gain[None], key_blocks, d_context[0])
    return (q_grad[None], k_grad[None], v_grad[None], gq[0], gk[0])


def solution(mesh):
    placed = (
        P("dp", "seq", None),
        P("dp", "seq", None),
        P("dp", "seq", None),
        P("dp"),
        P("dp"),
        P("seq", None, None),
        P("dp", "seq", None),
    )
    return jax.shard_map(
        functools.partial(shards, mesh.shape["seq"], mesh.shape["dp"]),
        mesh=mesh,
        in_specs=placed,
        out_specs=(
            P("dp", "seq", None),
            P("dp", "seq", None),
            P("dp", "seq", None),
            P("dp"),
            P("dp"),
        ),
        check_vma=False,
    )
```

```python
import functools
import math

import jax
import jax.numpy as jnp
from jax import lax
from jax.experimental import pallas as pl
from jax.experimental.pallas import tpu as pltpu
from jax.sharding import PartitionSpec as P

BLK = 128
GLOB = 1


EPSILON = 1e-06


def slot_keep(pattern):
    slot_count = pattern.shape[-1]
    present = pattern >= 0
    same_block = pattern[:, :, None] == pattern[:, None, :]
    earlier = jnp.arange(slot_count)[None, :] < jnp.arange(slot_count)[:, None]
    repeated = jnp.any(same_block & earlier[None, :, :], axis=2)
    return present & jnp.logical_not(repeated)


def norm_rows(raw_rows, gain_vec):
    length_total = raw_rows.shape[0]
    width = gain_vec.shape[0]
    values = raw_rows.astype(jnp.float32).reshape(length_total, -1, width)
    inverse = lax.rsqrt(jnp.mean(values * values, axis=-1, keepdims=True) + EPSILON)
    normed = (values * inverse * gain_vec).astype(jnp.bfloat16).reshape(length_total, -1)
    return (normed, inverse)


def norm_back(raw_rows, inverse, gain_vec, d_normed):
    length_total = raw_rows.shape[0]
    width = gain_vec.shape[0]
    values = raw_rows.astype(jnp.float32).reshape(length_total, -1, width)
    upstream = d_normed.astype(jnp.float32).reshape(length_total, -1, width)
    scaled = gain_vec * upstream
    row_total = jnp.sum(scaled * values, axis=-1, keepdims=True)
    d_raw = inverse * scaled - inverse * inverse * inverse * values * row_total / width
    gain_part = jnp.sum(upstream * values * inverse, axis=(0, 1))
    return (d_raw.astype(jnp.bfloat16).reshape(length_total, -1), gain_part)


def softmax_rows(score_matrix, axes):
    row_peak = jnp.max(score_matrix, axis=axes, keepdims=True)
    raised = jnp.exp(score_matrix - row_peak)
    return raised / jnp.sum(raised, axis=axes, keepdims=True)


def tile_layout(head_array):
    length_total, width_per_head = head_array.shape
    return head_array.reshape(length_total // BLK, BLK, width_per_head)


def group_size(blocks):
    return math.gcd(blocks, max(1, 1024 // BLK))


def backward_head(q_head, k_head, v_head, d_head, pattern):
    length_total, width_per_head = q_head.shape
    blocks = length_total // BLK
    lead_rows = GLOB * BLK
    logit_scale = 1.0 / math.sqrt(width_per_head)
    keep_slot = slot_keep(pattern)
    picked = jnp.maximum(pattern, 0)
    query_tiles = tile_layout(q_head)
    k_tiles = tile_layout(k_head)
    v_tiles = tile_layout(v_head)
    tile_gradient = tile_layout(d_head)
    group_len = group_size(blocks)
    top_precision = lax.Precision.HIGHEST

    def one_group(carry, group_index):
        k_acc, v_acc = carry
        first_block = group_index * group_len
        query_rows = lax.dynamic_slice_in_dim(query_tiles, first_block, group_len, 0)
        grad_rows = lax.dynamic_slice_in_dim(tile_gradient, first_block, group_len, 0)
        chosen = lax.dynamic_slice_in_dim(picked, first_block, group_len, 0)
        allowed = lax.dynamic_slice_in_dim(keep_slot, first_block, group_len, 0)
        selected_keys = k_tiles[chosen]
        selected_values = v_tiles[chosen]
        score_matrix = (
            jnp.einsum(
                "gqd,gskd->gqsk", query_rows, selected_keys, preferred_element_type=jnp.float32
            )
            * logit_scale
        )
        score_matrix = jnp.where(allowed[:, None, :, None], score_matrix, -jnp.inf)
        weights = softmax_rows(score_matrix, (2, 3))
        weight_reduced = weights.astype(jnp.bfloat16)
        sparse_query_row = (first_block + jnp.arange(group_len) >= GLOB)[:, None, None, None]
        weight_gradient = jnp.einsum(
            "gqd,gskd->gqsk", grad_rows, selected_values, preferred_element_type=jnp.float32
        )
        row_delta = jnp.sum(weights * weight_gradient, axis=(2, 3), keepdims=True)
        score_gradient = jnp.where(
            sparse_query_row, weights * (weight_gradient - row_delta) * logit_scale, 0.0
        ).astype(jnp.bfloat16)
        d_query = jnp.einsum(
            "gqsk,gskd->gqd", score_gradient, selected_keys, preferred_element_type=jnp.float32
        )
        key_pieces = jnp.einsum(
            "gqsk,gqd->gskd", score_gradient, query_rows, preferred_element_type=jnp.float32
        )
        kept_low = jnp.where(sparse_query_row, weight_reduced, jnp.zeros_like(weight_reduced))
        value_pieces = jnp.einsum(
            "gqsk,gqd->gskd", kept_low, grad_rows, preferred_element_type=jnp.float32
        )
        one_hot = (
            (chosen[:, :, None] == jnp.arange(blocks)[None, None, :]) & allowed[:, :, None]
        ).astype(jnp.float32)
        k_acc = k_acc + jnp.einsum("gsn,gskd->nkd", one_hot, key_pieces, precision=top_precision)
        v_acc = v_acc + jnp.einsum("gsn,gskd->nkd", one_hot, value_pieces, precision=top_precision)
        return ((k_acc, v_acc), d_query)

    zero_acc = jnp.zeros((blocks, BLK, width_per_head), jnp.float32)
    sums, q_groups = lax.scan(one_group, (zero_acc, zero_acc), jnp.arange(blocks // group_len))
    query_sparse = q_groups.reshape(length_total, width_per_head)
    k_sparse = sums[0].reshape(length_total, width_per_head)
    v_sparse = sums[1].reshape(length_total, width_per_head)
    q_lead = q_head[:lead_rows]
    d_lead = d_head[:lead_rows]
    lead_scores = (
        jnp.einsum("qd,kd->qk", q_lead, k_head, preferred_element_type=jnp.float32) * logit_scale
    )
    lead_weights = softmax_rows(lead_scores, (1,))
    lead_low = lead_weights.astype(jnp.bfloat16)
    lead_dprob = jnp.einsum("qd,kd->qk", d_lead, v_head, preferred_element_type=jnp.float32)
    lead_delta = jnp.sum(lead_weights * lead_dprob, axis=1, keepdims=True)
    lead_dscore = (lead_weights * (lead_dprob - lead_delta) * logit_scale).astype(jnp.bfloat16)
    lead_dq = jnp.dot(lead_dscore, k_head, preferred_element_type=jnp.float32)
    lead_dk = jnp.einsum("qk,qd->kd", lead_dscore, q_lead, preferred_element_type=jnp.float32)
    lead_dv = jnp.einsum("qk,qd->kd", lead_low, d_lead, preferred_element_type=jnp.float32)
    d_query = jnp.concatenate([lead_dq, query_sparse[lead_rows:]], axis=0).astype(jnp.bfloat16)
    return (d_query, k_sparse + lead_dk, v_sparse + lead_dv)


def widen_heads(rows, width_per_head, group_len):
    tokens = rows.shape[0]
    kv_count = rows.shape[1] // width_per_head
    spread = jnp.broadcast_to(
        rows.reshape(tokens, kv_count, 1, width_per_head),
        (tokens, kv_count, group_len, width_per_head),
    )
    return spread.reshape(tokens, kv_count * group_len * width_per_head)


def shards_by_head(q_raw, k_raw, v_raw, q_gain, k_gain, key_blocks, d_context):
    q_full, k_full = (
        lax.all_gather(q_gain, "dp", axis=0, tiled=True),
        lax.all_gather(k_gain, "dp", axis=0, tiled=True),
    )
    q_normed, q_inverse = norm_rows(q_raw[0], q_full)
    k_normed, k_inverse = norm_rows(k_raw[0], k_full)
    width_per_head = q_full.shape[0]
    group_len = q_raw.shape[2] // k_raw.shape[2]
    tokens = q_raw.shape[1]
    k_wide = widen_heads(k_normed, width_per_head, group_len)
    v_wide = widen_heads(v_raw[0], width_per_head, group_len)
    q_heads, k_heads, v_heads, d_heads = (
        lax.all_to_all(q_normed, "seq", split_axis=1, concat_axis=0, tiled=True),
        lax.all_to_all(k_wide, "seq", split_axis=1, concat_axis=0, tiled=True),
        lax.all_to_all(v_wide, "seq", split_axis=1, concat_axis=0, tiled=True),
        lax.all_to_all(d_context[0], "seq", split_axis=1, concat_axis=0, tiled=True),
    )
    length_total = q_heads.shape[0]
    head_count = key_blocks.shape[0]

    def split_heads(head_array):
        return head_array.reshape(length_total, head_count, width_per_head)

    def merge_heads(head_array):
        return head_array.reshape(length_total, head_count * width_per_head)

    backward = jax.vmap(backward_head, in_axes=(1, 1, 1, 1, 0), out_axes=1)
    dq_heads, dk_heads, dv_heads = backward(
        split_heads(q_heads),
        split_heads(k_heads),
        split_heads(v_heads),
        split_heads(d_heads),
        key_blocks,
    )
    dq_heads = merge_heads(dq_heads)
    dk_heads = merge_heads(dk_heads)
    dv_heads = merge_heads(dv_heads)
    d_q_normed = lax.all_to_all(dq_heads, "seq", split_axis=0, concat_axis=1, tiled=True)
    dk_terms, dv_terms = (
        lax.all_to_all(dk_heads, "seq", split_axis=0, concat_axis=1, tiled=True),
        lax.all_to_all(dv_heads, "seq", split_axis=0, concat_axis=1, tiled=True),
    )
    kv_count = k_raw.shape[2] // width_per_head
    d_k_normed = (
        jnp.sum(dk_terms.reshape(tokens, kv_count, group_len, width_per_head), axis=2)
        .astype(jnp.bfloat16)
        .reshape(tokens, kv_count * width_per_head)
    )
    v_grad = (
        jnp.sum(dv_terms.reshape(tokens, kv_count, group_len, width_per_head), axis=2)
        .astype(jnp.bfloat16)
        .reshape(tokens, kv_count * width_per_head)
    )
    q_grad, q_part = norm_back(q_raw[0], q_inverse, q_full, d_q_normed)
    k_grad, k_part = norm_back(k_raw[0], k_inverse, k_full, d_k_normed)
    q_total, k_total = lax.psum((q_part, k_part), ("seq", "dp"))
    shard_len = q_gain.shape[0]
    offset = lax.axis_index("dp") * shard_len
    q_gain_grad = lax.dynamic_slice_in_dim(q_total, offset, shard_len)
    k_gain_grad = lax.dynamic_slice_in_dim(k_total, offset, shard_len)
    return (q_grad[None], k_grad[None], v_grad[None], q_gain_grad, k_gain_grad)


F32 = jnp.float32
BF16 = jnp.bfloat16
MESH = pl.DeviceIdType.MESH
VMEM_ROOM = 56 * 1024 * 1024


def token_kernel(
    n, dpn,
    q_in, k_in, v_in, gq_in, gk_in, kb_in, d_in,
    q_out, k_out, v_out, gq_out, gk_out,
    q_s, d_s, k_all, v_all, kb_all, kbm, gq_all, gk_all, bias,
    q_hat, q_inv, q_st, q_tr, d_st, d_tr, k_hat, k_tr,
    s_scr, p_scr, ds_scr, acc, sib_out, sib_in, chip_out, chip_in,
    part1, part2,
    loc, k_snd, k_rcv, v_snd, v_rcv, kf_snd, kf_rcv, vf_snd, vf_rcv,
    b_snd, b_rcv, gq_snd, gq_rcv, gk_snd, gk_rcv,
    s_snd, s_rcv, x_snd, x_rcv, p1_snd, p1_rcv, p2_snd, p2_rcv,
):
    nc = n // 2
    hd = q_hat.shape[2]
    tokens = q_s.shape[0]
    heads = q_s.shape[1] // hd
    groups = k_in.shape[1] // hd
    per = heads // groups
    wide = per * tokens
    scale = 1.0 / math.sqrt(hd)
    raise_by = scale * math.log2(math.e)

    me = lax.axis_index("seq")
    md = lax.axis_index("dp")
    core = lax.rem(me, 2)
    chip = lax.div(me, 2)
    sib = 2 * chip + 1 - core

    def src_chip(t):
        return lax.rem(chip + nc - t, nc)

    def dst_chip(t):
        return lax.rem(chip + t, nc)

    def send(src, dst, snd, rcv, **where):
        return pltpu.make_async_remote_copy(
            src_ref=src, dst_ref=dst, send_sem=snd, recv_sem=rcv,
            device_id=where, device_id_type=MESH,
        )

    def local(src, dst, i):
        copy = pltpu.make_async_copy(src, dst, loc.at[i])
        copy.start()
        return copy

    def cols_of(ref, g):
        return ref.at[:, g * hd:(g + 1) * hd]

    own_k = [local(cols_of(k_in, g), k_all.at[g, me], 7 + g) for g in range(groups)]
    own_v = [local(cols_of(v_in, g), v_all.at[g, me], 7 + groups + g) for g in range(groups)]
    own_gq = local(gq_in, gq_all.at[md], 2)
    own_gk = local(gk_in, gk_all.at[md], 3)
    own_kb = local(kb_in, kb_all.at[me], 4)
    own_q = local(q_in, q_s, 5)
    own_d = local(d_in, d_s, 6)

    barrier = pltpu.get_barrier_semaphore()
    for r in range(1, n):
        pl.semaphore_signal(barrier, inc=1, device_id={"seq": lax.rem(me + r, n)}, device_id_type=MESH)
    for r in range(1, dpn):
        pl.semaphore_signal(barrier, inc=1, device_id={"dp": lax.rem(md + r, dpn)}, device_id_type=MESH)
    pl.semaphore_wait(barrier, n - 1 + dpn - 1)

    pending = []

    def go(copy):
        copy.start()
        pending.append(copy)

    for r in range(1, dpn):
        to = lax.rem(md + r, dpn)
        go(send(gq_in, gq_all.at[md], gq_snd.at[r], gq_rcv.at[r], dp=to))
        go(send(gk_in, gk_all.at[md], gk_snd.at[r], gk_rcv.at[r], dp=to))
    def spread(g):
        for ref, held_in, snd, rcv in ((k_in, k_all, k_snd, k_rcv), (v_in, v_all, v_snd, v_rcv)):
            for t in range(1, nc):
                go(send(cols_of(ref, g), held_in.at[g, me], snd.at[g, t], rcv.at[g, t], seq=2 * dst_chip(t) + core))
            go(send(cols_of(ref, g), held_in.at[g, me], snd.at[g, 0], rcv.at[g, 0], seq=sib))

    spread(0)
    for r in range(1, n):
        go(send(kb_in, kb_all.at[me], b_snd.at[r], b_rcv.at[r], seq=lax.rem(me + r, n)))
    for g in range(1, groups):
        spread(g)

    def arrived(ref, snd, rcv):
        send(ref, ref, snd, rcv, seq=sib).wait_recv()

    own_d.wait()
    for h in range(heads):
        g, i = h // per, h % per
        rows = slice(i * tokens, (i + 1) * tokens)
        x = d_s[:, h * hd:(h + 1) * hd]
        d_st[g, rows, :] = x
        d_tr[g, :, rows] = x.astype(F32).T.astype(BF16)
    own_q.wait()
    for h in range(heads):
        x = q_s[:, h * hd:(h + 1) * hd].astype(F32)
        inv = lax.rsqrt(jnp.mean(x * x, axis=1, keepdims=True) + EPSILON)
        inv = jnp.broadcast_to(inv, (tokens, hd))
        q_inv[h] = inv
        q_hat[h] = x * inv

    def forward(g, t):
        frm = 2 * src_chip(t) + core
        for held_in, snd, rcv, f_snd, f_rcv in (
            (k_all, k_snd, k_rcv, kf_snd, kf_rcv), (v_all, v_snd, v_rcv, vf_snd, vf_rcv),
        ):
            ref = held_in.at[g, frm]
            arrived(ref, snd.at[g, t], rcv.at[g, t])
            go(send(ref, ref, f_snd.at[g, t], f_rcv.at[g, t], seq=sib))

    for t in range(1, nc):
        forward(0, t)

    own_gq.wait()
    own_gk.wait()
    for r in range(1, dpn):
        frm = lax.rem(md + dpn - r, dpn)
        arrived(gq_all.at[frm], gq_snd.at[r], gq_rcv.at[r])
        arrived(gk_all.at[frm], gk_snd.at[r], gk_rcv.at[r])
    q_gain = jnp.concatenate([gq_all[i] for i in range(dpn)], axis=1)
    k_gain = jnp.concatenate([gk_all[i] for i in range(dpn)], axis=1)

    def query_tiles(g):
        for i in range(per):
            rows = slice(i * tokens, (i + 1) * tokens)
            x = q_hat[g * per + i] * q_gain
            q_st[g, rows, :] = x.astype(BF16)
            q_tr[g, :, rows] = x.T.astype(BF16)

    query_tiles(0)
    own_kb.wait()
    for r in range(1, n):
        arrived(kb_all.at[lax.rem(me + n - r, n)], b_snd.at[r], b_rcv.at[r])
    held = kb_all.shape[2]
    for h in range(heads):
        kbm[h] = kb_all[h // held, :, h % held, :].astype(F32)
    lane = lax.broadcasted_iota(jnp.int32, kbm.shape, 2)
    named = jnp.max(jnp.where(lane == me, kbm[...], -1.0), axis=2, keepdims=True)
    for j in range(n):
        hit = jnp.where((named == float(j)) | (me < GLOB), 0.0, -jnp.inf)
        bias[j] = jnp.broadcast_to(jnp.max(hit, axis=1, keepdims=True), (heads, 1, tokens))

    def pair(g, t, peak):
        at = src_chip(t)
        if t == 0:
            own_k[g].wait()
            arrived(k_all.at[g, sib], k_snd.at[g, 0], k_rcv.at[g, 0])
        else:
            arrived(k_all.at[g, 2 * at + 1 - core], kf_snd.at[g, t], kf_rcv.at[g, t])
        x = k_all[g, pl.ds(2 * at, 2)].reshape(2 * tokens, hd).astype(F32)
        inv = lax.rsqrt(jnp.mean(x * x, axis=1, keepdims=True) + EPSILON)
        x = x * inv
        k_hat[t, g] = x
        x = x * k_gain
        k_tr[t, g] = x.T.astype(BF16)
        s = jnp.dot(x.astype(BF16), q_tr[g], preferred_element_type=F32)
        for i in range(2):
            line = jnp.concatenate([bias[2 * at + i, h] for h in range(g * per, (g + 1) * per)], axis=1)
            part = s[i * tokens:(i + 1) * tokens] + line
            s_scr[t, g, i * tokens:(i + 1) * tokens, :] = part
            peak = jnp.maximum(peak, jnp.max(part, axis=0, keepdims=True))
        if t == 0:
            own_v[g].wait()
            arrived(v_all.at[g, sib], v_snd.at[g, 0], v_rcv.at[g, 0])
        else:
            arrived(v_all.at[g, 2 * at + 1 - core], vf_snd.at[g, t], vf_rcv.at[g, t])
        vals = v_all[g, pl.ds(2 * at, 2)].reshape(2 * tokens, hd)
        p_scr[t, g] = jnp.dot(vals, d_tr[g], preferred_element_type=F32)
        return peak

    def hand_on(g, t):
        arrived(sib_in.at[g, t], s_snd.at[g, t], s_rcv.at[g, t])
        chip_out[g, t] = (acc[g, t, core] + sib_in[g, t].astype(F32)).astype(BF16)
        go(send(chip_out.at[g, t], chip_in.at[g, t], x_snd.at[g, t], x_rcv.at[g, t], seq=2 * src_chip(t) + core))

    k_part = jnp.zeros((1, hd), F32)
    order = list(range(1, nc)) + [0]
    waiting = []
    for g in range(groups):
        peak = jnp.full((1, wide), -jnp.inf, F32)
        for t in range(nc):
            peak = pair(g, t, peak)
            if t == 0:
                while waiting:
                    hand_on(*waiting.pop(0))
        if g + 1 < groups:
            for t in range(1, nc):
                forward(g + 1, t)
            query_tiles(g + 1)
        total = jnp.zeros((1, wide), F32)
        cross = jnp.zeros((1, wide), F32)
        for t in range(nc):
            e = jnp.exp2((s_scr[t, g] - peak) * raise_by)
            s_scr[t, g] = e
            total = total + jnp.sum(e, axis=0, keepdims=True)
            cross = cross + jnp.sum(e * p_scr[t, g], axis=0, keepdims=True)
        norm = 1.0 / total
        delta = cross * norm
        for t in order:
            w = s_scr[t, g] * norm
            ds = (w * (p_scr[t, g] - delta) * scale).astype(BF16)
            ds_scr[t, g] = ds
            dk = jnp.dot(ds, q_st[g], preferred_element_type=F32)
            dv = jnp.dot(w.astype(BF16), d_st[g], preferred_element_type=F32)
            for i in range(2):
                acc[g, t, i, 0] = dk[i * tokens:(i + 1) * tokens]
                acc[g, t, i, 1] = dv[i * tokens:(i + 1) * tokens]
            k_part = k_part + jnp.sum(dk * k_hat[t, g], axis=0, keepdims=True)
            sib_out[g, t] = acc[g, t, 1 - core].astype(BF16)
            go(send(sib_out.at[g, t], sib_in.at[g, t], s_snd.at[g, t], s_rcv.at[g, t], seq=sib))
            if waiting:
                hand_on(*waiting.pop(0))
            if t != 0:
                waiting.append((g, t))

    q_part = jnp.zeros((1, hd), F32)
    for g in range(groups):
        dq_tr = jnp.zeros((hd, wide), F32)
        for t in range(nc):
            dq_tr = dq_tr + jnp.dot(k_tr[t, g], ds_scr[t, g], preferred_element_type=F32)
        while waiting:
            hand_on(*waiting.pop(0))
        for i in range(per):
            h = g * per + i
            dq = dq_tr[:, i * tokens:(i + 1) * tokens].T.astype(BF16).astype(F32)
            x = q_hat[h]
            q_part = q_part + jnp.sum(dq * x, axis=0, keepdims=True)
            y = dq * q_gain
            mean = jnp.mean(y * x, axis=1, keepdims=True)
            q_out[:, h * hd:(h + 1) * hd] = (q_inv[h] * (y - x * mean)).astype(BF16)

    part1[md] = jnp.concatenate([q_part, k_part, jnp.zeros((6, hd), F32)], axis=0)
    for r in range(1, dpn):
        go(send(part1.at[md], part1.at[md], p1_snd.at[r], p1_rcv.at[r], dp=lax.rem(md + r, dpn)))
    totals = []
    for g in range(groups):
        arrived(sib_in.at[g, 0], s_snd.at[g, 0], s_rcv.at[g, 0])
        totals.append(acc[g, 0, core] + sib_in[g, 0].astype(F32))
    for r in range(1, dpn):
        arrived(part1.at[lax.rem(md + dpn - r, dpn)], p1_snd.at[r], p1_rcv.at[r])
    gains = part1[0]
    for i in range(1, dpn):
        gains = gains + part1[i]
    part2[me] = gains
    for r in range(1, n):
        go(send(part2.at[me], part2.at[me], p2_snd.at[r], p2_rcv.at[r], seq=lax.rem(me + r, n)))

    for g in range(groups):
        total = totals[g]
        for t in range(1, nc):
            arrived(chip_in.at[g, t], x_snd.at[g, t], x_rcv.at[g, t])
            total = total + chip_in[g, t].astype(F32)
        cols = slice(g * hd, (g + 1) * hd)
        v_out[:, cols] = total[1].astype(BF16)
        x = k_all[g, me].astype(F32)
        inv = lax.rsqrt(jnp.mean(x * x, axis=1, keepdims=True) + EPSILON)
        x = x * inv
        y = total[0].astype(BF16).astype(F32) * k_gain
        mean = jnp.mean(y * x, axis=1, keepdims=True)
        k_out[:, cols] = (inv * (y - x * mean)).astype(BF16)

    for r in range(1, n):
        arrived(part2.at[lax.rem(me + n - r, n)], p2_snd.at[r], p2_rcv.at[r])
    gains = part2[0]
    for i in range(1, n):
        gains = gains + part2[i]
    share = hd // dpn
    mine = jnp.zeros((8, share), F32)
    for i in range(dpn):
        mine = mine + jnp.where(md == i, gains[:, i * share:(i + 1) * share], 0.0)
    gq_out[...] = mine[0:1]
    gk_out[...] = mine[1:2]

    for copy in pending:
        copy.wait_send()


def store_kernel(*refs):
    sems = refs[10]
    copies = [pltpu.make_async_copy(refs[i], refs[5 + i], sems.at[i]) for i in range(5)]
    for copy in copies:
        copy.start()
    for copy in copies:
        copy.wait()


def scratch_list(n, dpn, tokens, hd, heads, groups, held, blocks, slots):
    nc = n // 2
    wide = heads // groups * tokens
    vm = pltpu.VMEM
    dma = pltpu.SemaphoreType.DMA
    arrays = [
        vm((tokens, heads * hd), BF16),
        vm((tokens, heads * hd), BF16),
        vm((groups, n, tokens, hd), BF16),
        vm((groups, n, tokens, hd), BF16),
        vm((n, slots, held, blocks), jnp.int32),
        vm((heads, slots, blocks), F32),
        vm((dpn, 1, hd // dpn), F32),
        vm((dpn, 1, hd // dpn), F32),
        vm((n, heads, 1, tokens), F32),
        vm((heads, tokens, hd), F32),
        vm((heads, tokens, hd), F32),
        vm((groups, wide, hd), BF16),
        vm((groups, hd, wide), BF16),
        vm((groups, wide, hd), BF16),
        vm((groups, hd, wide), BF16),
        vm((nc, groups, 2 * tokens, hd), F32),
        vm((nc, groups, hd, 2 * tokens), BF16),
        vm((nc, groups, 2 * tokens, wide), F32),
        vm((nc, groups, 2 * tokens, wide), F32),
        vm((nc, groups, 2 * tokens, wide), BF16),
        vm((groups, nc, 2, 2, tokens, hd), F32),
        vm((groups, nc, 2, tokens, hd), BF16),
        vm((groups, nc, 2, tokens, hd), BF16),
        vm((groups, nc, 2, tokens, hd), BF16),
        vm((groups, nc, 2, tokens, hd), BF16),
        vm((dpn, 8, hd), F32),
        vm((n, 8, hd), F32),
    ]
    sems = [dma((7 + 2 * groups,))] + [dma((groups, nc))] * 8 + [dma((n,))] * 2 + [dma((dpn,))] * 4
    sems += [dma((groups, nc))] * 4 + [dma((dpn,))] * 2 + [dma((n,))] * 2
    return arrays, sems


def shards(n, dpn, q_raw, k_raw, v_raw, q_gain, k_gain, key_blocks, d_context):
    hd = q_gain.shape[0] * dpn
    tokens = q_raw.shape[1]
    heads = q_raw.shape[2] // hd
    groups = k_raw.shape[2] // hd
    held, blocks, slots = key_blocks.shape
    arrays, sems = scratch_list(n, dpn, tokens, hd, heads, groups, held, blocks, slots)
    room = sum(math.prod(a.shape) * jnp.dtype(a.dtype).itemsize for a in arrays)
    fits = room < VMEM_ROOM - 16 * 1024 * 1024
    if n % 2 or tokens != BLK or q_raw.shape[0] != 1 or not fits:
        return shards_by_head(q_raw, k_raw, v_raw, q_gain, k_gain, key_blocks, d_context)
    anywhere = pl.BlockSpec(memory_space=pl.ANY)
    vmem = pl.BlockSpec(memory_space=pltpu.VMEM)
    share = hd // dpn
    kvd = groups * hd
    q_grad, k_grad, v_grad, gq, gk = pl.pallas_call(
        functools.partial(token_kernel, n, dpn),
        out_shape=(
            pltpu.VMEM((tokens, heads * hd), BF16),
            pltpu.VMEM((tokens, kvd), BF16),
            pltpu.VMEM((tokens, kvd), BF16),
            pltpu.VMEM((1, share), F32),
            pltpu.VMEM((1, share), F32),
        ),
        in_specs=[anywhere] * 7,
        out_specs=(vmem,) * 5,
        scratch_shapes=arrays + sems,
        compiler_params=pltpu.CompilerParams(
            collective_id=0, has_side_effects=True, vmem_limit_bytes=VMEM_ROOM
        ),
    )(q_raw[0], k_raw[0], v_raw[0], q_gain[None], k_gain[None], key_blocks.transpose(2, 0, 1), d_context[0])
    done = (q_grad, k_grad, v_grad, gq, gk)
    done = pl.pallas_call(
        store_kernel,
        out_shape=tuple(jax.ShapeDtypeStruct(x.shape, x.dtype) for x in done),
        in_specs=[vmem] * 5,
        out_specs=(anywhere,) * 5,
        scratch_shapes=[pltpu.SemaphoreType.DMA((5,))],
        compiler_params=pltpu.CompilerParams(vmem_limit_bytes=4 * 1024 * 1024),
    )(*done)
    return (done[0][None], done[1][None], done[2][None], done[3][0], done[4][0])


def solution(mesh):
    placed = (
        P("dp", "seq", None),
        P("dp", "seq", None),
        P("dp", "seq", None),
        P("dp"),
        P("dp"),
        P("seq", None, None),
        P("dp", "seq", None),
    )
    return jax.shard_map(
        functools.partial(shards, mesh.shape["seq"], mesh.shape["dp"]),
        mesh=mesh,
        in_specs=placed,
        out_specs=(
            P("dp", "seq", None),
            P("dp", "seq", None),
            P("dp", "seq", None),
            P("dp"),
            P("dp"),
        ),
        check_vma=False,
    )
```

```python
import functools
import math

import jax
import jax.numpy as jnp
from jax import lax
from jax.experimental import pallas as pl
from jax.experimental.pallas import tpu as pltpu
from jax.sharding import PartitionSpec as P

BLK = 128
GLOB = 1


EPSILON = 1e-06


def slot_keep(pattern):
    slot_count = pattern.shape[-1]
    present = pattern >= 0
    same_block = pattern[:, :, None] == pattern[:, None, :]
    earlier = jnp.arange(slot_count)[None, :] < jnp.arange(slot_count)[:, None]
    repeated = jnp.any(same_block & earlier[None, :, :], axis=2)
    return present & jnp.logical_not(repeated)


def norm_rows(raw_rows, gain_vec):
    length_total = raw_rows.shape[0]
    width = gain_vec.shape[0]
    values = raw_rows.astype(jnp.float32).reshape(length_total, -1, width)
    inverse = lax.rsqrt(jnp.mean(values * values, axis=-1, keepdims=True) + EPSILON)
    normed = (values * inverse * gain_vec).astype(jnp.bfloat16).reshape(length_total, -1)
    return (normed, inverse)


def norm_back(raw_rows, inverse, gain_vec, d_normed):
    length_total = raw_rows.shape[0]
    width = gain_vec.shape[0]
    values = raw_rows.astype(jnp.float32).reshape(length_total, -1, width)
    upstream = d_normed.astype(jnp.float32).reshape(length_total, -1, width)
    scaled = gain_vec * upstream
    row_total = jnp.sum(scaled * values, axis=-1, keepdims=True)
    d_raw = inverse * scaled - inverse * inverse * inverse * values * row_total / width
    gain_part = jnp.sum(upstream * values * inverse, axis=(0, 1))
    return (d_raw.astype(jnp.bfloat16).reshape(length_total, -1), gain_part)


def softmax_rows(score_matrix, axes):
    row_peak = jnp.max(score_matrix, axis=axes, keepdims=True)
    raised = jnp.exp(score_matrix - row_peak)
    return raised / jnp.sum(raised, axis=axes, keepdims=True)


def tile_layout(head_array):
    length_total, width_per_head = head_array.shape
    return head_array.reshape(length_total // BLK, BLK, width_per_head)


def group_size(blocks):
    return math.gcd(blocks, max(1, 1024 // BLK))


def backward_head(q_head, k_head, v_head, d_head, pattern):
    length_total, width_per_head = q_head.shape
    blocks = length_total // BLK
    lead_rows = GLOB * BLK
    logit_scale = 1.0 / math.sqrt(width_per_head)
    keep_slot = slot_keep(pattern)
    picked = jnp.maximum(pattern, 0)
    query_tiles = tile_layout(q_head)
    k_tiles = tile_layout(k_head)
    v_tiles = tile_layout(v_head)
    tile_gradient = tile_layout(d_head)
    group_len = group_size(blocks)
    top_precision = lax.Precision.HIGHEST

    def one_group(carry, group_index):
        k_acc, v_acc = carry
        first_block = group_index * group_len
        query_rows = lax.dynamic_slice_in_dim(query_tiles, first_block, group_len, 0)
        grad_rows = lax.dynamic_slice_in_dim(tile_gradient, first_block, group_len, 0)
        chosen = lax.dynamic_slice_in_dim(picked, first_block, group_len, 0)
        allowed = lax.dynamic_slice_in_dim(keep_slot, first_block, group_len, 0)
        selected_keys = k_tiles[chosen]
        selected_values = v_tiles[chosen]
        score_matrix = (
            jnp.einsum(
                "gqd,gskd->gqsk", query_rows, selected_keys, preferred_element_type=jnp.float32
            )
            * logit_scale
        )
        score_matrix = jnp.where(allowed[:, None, :, None], score_matrix, -jnp.inf)
        weights = softmax_rows(score_matrix, (2, 3))
        weight_reduced = weights.astype(jnp.bfloat16)
        sparse_query_row = (first_block + jnp.arange(group_len) >= GLOB)[:, None, None, None]
        weight_gradient = jnp.einsum(
            "gqd,gskd->gqsk", grad_rows, selected_values, preferred_element_type=jnp.float32
        )
        row_delta = jnp.sum(weights * weight_gradient, axis=(2, 3), keepdims=True)
        score_gradient = jnp.where(
            sparse_query_row, weights * (weight_gradient - row_delta) * logit_scale, 0.0
        ).astype(jnp.bfloat16)
        d_query = jnp.einsum(
            "gqsk,gskd->gqd", score_gradient, selected_keys, preferred_element_type=jnp.float32
        )
        key_pieces = jnp.einsum(
            "gqsk,gqd->gskd", score_gradient, query_rows, preferred_element_type=jnp.float32
        )
        kept_low = jnp.where(sparse_query_row, weight_reduced, jnp.zeros_like(weight_reduced))
        value_pieces = jnp.einsum(
            "gqsk,gqd->gskd", kept_low, grad_rows, preferred_element_type=jnp.float32
        )
        one_hot = (
            (chosen[:, :, None] == jnp.arange(blocks)[None, None, :]) & allowed[:, :, None]
        ).astype(jnp.float32)
        k_acc = k_acc + jnp.einsum("gsn,gskd->nkd", one_hot, key_pieces, precision=top_precision)
        v_acc = v_acc + jnp.einsum("gsn,gskd->nkd", one_hot, value_pieces, precision=top_precision)
        return ((k_acc, v_acc), d_query)

    zero_acc = jnp.zeros((blocks, BLK, width_per_head), jnp.float32)
    sums, q_groups = lax.scan(one_group, (zero_acc, zero_acc), jnp.arange(blocks // group_len))
    query_sparse = q_groups.reshape(length_total, width_per_head)
    k_sparse = sums[0].reshape(length_total, width_per_head)
    v_sparse = sums[1].reshape(length_total, width_per_head)
    q_lead = q_head[:lead_rows]
    d_lead = d_head[:lead_rows]
    lead_scores = (
        jnp.einsum("qd,kd->qk", q_lead, k_head, preferred_element_type=jnp.float32) * logit_scale
    )
    lead_weights = softmax_rows(lead_scores, (1,))
    lead_low = lead_weights.astype(jnp.bfloat16)
    lead_dprob = jnp.einsum("qd,kd->qk", d_lead, v_head, preferred_element_type=jnp.float32)
    lead_delta = jnp.sum(lead_weights * lead_dprob, axis=1, keepdims=True)
    lead_dscore = (lead_weights * (lead_dprob - lead_delta) * logit_scale).astype(jnp.bfloat16)
    lead_dq = jnp.dot(lead_dscore, k_head, preferred_element_type=jnp.float32)
    lead_dk = jnp.einsum("qk,qd->kd", lead_dscore, q_lead, preferred_element_type=jnp.float32)
    lead_dv = jnp.einsum("qk,qd->kd", lead_low, d_lead, preferred_element_type=jnp.float32)
    d_query = jnp.concatenate([lead_dq, query_sparse[lead_rows:]], axis=0).astype(jnp.bfloat16)
    return (d_query, k_sparse + lead_dk, v_sparse + lead_dv)


def widen_heads(rows, width_per_head, group_len):
    tokens = rows.shape[0]
    kv_count = rows.shape[1] // width_per_head
    spread = jnp.broadcast_to(
        rows.reshape(tokens, kv_count, 1, width_per_head),
        (tokens, kv_count, group_len, width_per_head),
    )
    return spread.reshape(tokens, kv_count * group_len * width_per_head)


def shards_by_head(q_raw, k_raw, v_raw, q_gain, k_gain, key_blocks, d_context):
    q_full, k_full = (
        lax.all_gather(q_gain, "dp", axis=0, tiled=True),
        lax.all_gather(k_gain, "dp", axis=0, tiled=True),
    )
    q_normed, q_inverse = norm_rows(q_raw[0], q_full)
    k_normed, k_inverse = norm_rows(k_raw[0], k_full)
    width_per_head = q_full.shape[0]
    group_len = q_raw.shape[2] // k_raw.shape[2]
    tokens = q_raw.shape[1]
    k_wide = widen_heads(k_normed, width_per_head, group_len)
    v_wide = widen_heads(v_raw[0], width_per_head, group_len)
    q_heads, k_heads, v_heads, d_heads = (
        lax.all_to_all(q_normed, "seq", split_axis=1, concat_axis=0, tiled=True),
        lax.all_to_all(k_wide, "seq", split_axis=1, concat_axis=0, tiled=True),
        lax.all_to_all(v_wide, "seq", split_axis=1, concat_axis=0, tiled=True),
        lax.all_to_all(d_context[0], "seq", split_axis=1, concat_axis=0, tiled=True),
    )
    length_total = q_heads.shape[0]
    head_count = key_blocks.shape[0]

    def split_heads(head_array):
        return head_array.reshape(length_total, head_count, width_per_head)

    def merge_heads(head_array):
        return head_array.reshape(length_total, head_count * width_per_head)

    backward = jax.vmap(backward_head, in_axes=(1, 1, 1, 1, 0), out_axes=1)
    dq_heads, dk_heads, dv_heads = backward(
        split_heads(q_heads),
        split_heads(k_heads),
        split_heads(v_heads),
        split_heads(d_heads),
        key_blocks,
    )
    dq_heads = merge_heads(dq_heads)
    dk_heads = merge_heads(dk_heads)
    dv_heads = merge_heads(dv_heads)
    d_q_normed = lax.all_to_all(dq_heads, "seq", split_axis=0, concat_axis=1, tiled=True)
    dk_terms, dv_terms = (
        lax.all_to_all(dk_heads, "seq", split_axis=0, concat_axis=1, tiled=True),
        lax.all_to_all(dv_heads, "seq", split_axis=0, concat_axis=1, tiled=True),
    )
    kv_count = k_raw.shape[2] // width_per_head
    d_k_normed = (
        jnp.sum(dk_terms.reshape(tokens, kv_count, group_len, width_per_head), axis=2)
        .astype(jnp.bfloat16)
        .reshape(tokens, kv_count * width_per_head)
    )
    v_grad = (
        jnp.sum(dv_terms.reshape(tokens, kv_count, group_len, width_per_head), axis=2)
        .astype(jnp.bfloat16)
        .reshape(tokens, kv_count * width_per_head)
    )
    q_grad, q_part = norm_back(q_raw[0], q_inverse, q_full, d_q_normed)
    k_grad, k_part = norm_back(k_raw[0], k_inverse, k_full, d_k_normed)
    q_total, k_total = lax.psum((q_part, k_part), ("seq", "dp"))
    shard_len = q_gain.shape[0]
    offset = lax.axis_index("dp") * shard_len
    q_gain_grad = lax.dynamic_slice_in_dim(q_total, offset, shard_len)
    k_gain_grad = lax.dynamic_slice_in_dim(k_total, offset, shard_len)
    return (q_grad[None], k_grad[None], v_grad[None], q_gain_grad, k_gain_grad)


F32 = jnp.float32
BF16 = jnp.bfloat16
MESH = pl.DeviceIdType.MESH
CHUNK = 32
VMEM_ROOM = 56 * 1024 * 1024


def fold_rows(tile):
    return jnp.sum(tile.reshape(tile.shape[0] // 8, 8, tile.shape[1]), axis=0)


def token_kernel(
    n, dpn,
    q_in, k_in, v_in, gq_in, gk_in, kb_in, d_in,
    q_out, k_out, v_out, gq_out, gk_out,
    q_s, d_s, k_all, v_all, kb_all, kbm, gq_all, gk_all, bias,
    q_hat, q_inv, q_st, q_tr, d_st, d_tr, k_hat, k_tr,
    s_scr, p_scr, ds_scr, w_scr, acc, sib_out, sib_in, chip_out, chip_in,
    part1, part2,
    loc, k_snd, k_rcv, v_snd, v_rcv, kf_snd, kf_rcv, vf_snd, vf_rcv,
    b_snd, b_rcv, gq_snd, gq_rcv, gk_snd, gk_rcv,
    s_snd, s_rcv, x_snd, x_rcv, p1_snd, p1_rcv, p2_snd, p2_rcv,
):
    nc = n // 2
    hd = q_hat.shape[2]
    tokens = q_s.shape[0]
    heads = q_s.shape[1] // hd
    groups = k_in.shape[1] // hd
    per = heads // groups
    wide = per * tokens
    scale = 1.0 / math.sqrt(hd)
    raise_by = scale * math.log2(math.e)

    me = lax.axis_index("seq")
    md = lax.axis_index("dp")
    core = lax.rem(me, 2)
    chip = lax.div(me, 2)
    sib = 2 * chip + 1 - core

    def src_chip(t):
        return lax.rem(chip + nc - t, nc)

    def dst_chip(t):
        return lax.rem(chip + t, nc)

    def send(src, dst, snd, rcv, **where):
        return pltpu.make_async_remote_copy(
            src_ref=src, dst_ref=dst, send_sem=snd, recv_sem=rcv,
            device_id=where, device_id_type=MESH,
        )

    def local(src, dst, i):
        copy = pltpu.make_async_copy(src, dst, loc.at[i])
        copy.start()
        return copy

    def cols_of(ref, g):
        return ref.at[:, g * hd:(g + 1) * hd]

    own_k = [local(cols_of(k_in, g), k_all.at[g, me], 7 + g) for g in range(groups)]
    own_v = [local(cols_of(v_in, g), v_all.at[g, me], 7 + groups + g) for g in range(groups)]
    own_gq = local(gq_in, gq_all.at[md], 2)
    own_gk = local(gk_in, gk_all.at[md], 3)
    own_kb = local(kb_in, kb_all.at[me], 4)
    own_q = local(q_in, q_s, 5)
    own_d = local(d_in, d_s, 6)

    barrier = pltpu.get_barrier_semaphore()
    for r in range(1, n):
        pl.semaphore_signal(barrier, inc=1, device_id={"seq": lax.rem(me + r, n)}, device_id_type=MESH)
    for r in range(1, dpn):
        pl.semaphore_signal(barrier, inc=1, device_id={"dp": lax.rem(md + r, dpn)}, device_id_type=MESH)
    own_d.wait()
    for h in range(heads):
        g, i = h // per, h % per
        rows = slice(i * tokens, (i + 1) * tokens)
        x = d_s[:, h * hd:(h + 1) * hd]
        d_st[g, rows, :] = x
        d_tr[g, :, rows] = x.astype(F32).T.astype(BF16)
    pl.semaphore_wait(barrier, n - 1 + dpn - 1)

    pending = []

    def go(copy):
        copy.start()
        pending.append(copy)

    for r in range(1, dpn):
        to = lax.rem(md + r, dpn)
        go(send(gq_in, gq_all.at[md], gq_snd.at[r], gq_rcv.at[r], dp=to))
        go(send(gk_in, gk_all.at[md], gk_snd.at[r], gk_rcv.at[r], dp=to))
    def spread(g):
        for ref, held_in, snd, rcv in ((k_in, k_all, k_snd, k_rcv), (v_in, v_all, v_snd, v_rcv)):
            for t in range(1, nc):
                go(send(cols_of(ref, g), held_in.at[g, me], snd.at[g, t], rcv.at[g, t], seq=2 * dst_chip(t) + core))
            go(send(cols_of(ref, g), held_in.at[g, me], snd.at[g, 0], rcv.at[g, 0], seq=sib))

    spread(0)
    for r in range(1, n):
        go(send(kb_in, kb_all.at[me], b_snd.at[r], b_rcv.at[r], seq=lax.rem(me + r, n)))
    for g in range(1, groups):
        spread(g)

    def arrived(ref, snd, rcv):
        send(ref, ref, snd, rcv, seq=sib).wait_recv()

    own_q.wait()
    for h in range(heads):
        x = q_s[:, h * hd:(h + 1) * hd].astype(F32)
        inv = lax.rsqrt(jnp.mean(x * x, axis=1, keepdims=True) + EPSILON)
        inv = jnp.broadcast_to(inv, (tokens, hd))
        q_inv[h] = inv
        q_hat[h] = x * inv

    def forward(g, t):
        frm = 2 * src_chip(t) + core
        for held_in, snd, rcv, f_snd, f_rcv in (
            (k_all, k_snd, k_rcv, kf_snd, kf_rcv), (v_all, v_snd, v_rcv, vf_snd, vf_rcv),
        ):
            ref = held_in.at[g, frm]
            arrived(ref, snd.at[g, t], rcv.at[g, t])
            go(send(ref, ref, f_snd.at[g, t], f_rcv.at[g, t], seq=sib))

    own_gq.wait()
    own_gk.wait()
    for r in range(1, dpn):
        frm = lax.rem(md + dpn - r, dpn)
        arrived(gq_all.at[frm], gq_snd.at[r], gq_rcv.at[r])
        arrived(gk_all.at[frm], gk_snd.at[r], gk_rcv.at[r])
    q_gain = jnp.concatenate([gq_all[i] for i in range(dpn)], axis=1)
    k_gain = jnp.concatenate([gk_all[i] for i in range(dpn)], axis=1)

    def query_tiles(g):
        for i in range(per):
            rows = slice(i * tokens, (i + 1) * tokens)
            x = q_hat[g * per + i] * q_gain
            q_st[g, rows, :] = x.astype(BF16)
            q_tr[g, :, rows] = x.T.astype(BF16)

    query_tiles(0)
    own_kb.wait()
    for r in range(1, n):
        arrived(kb_all.at[lax.rem(me + n - r, n)], b_snd.at[r], b_rcv.at[r])
    held = kb_all.shape[2]
    for h in range(heads):
        kbm[h] = kb_all[h // held, :, h % held, :].astype(F32)
    lane = lax.broadcasted_iota(jnp.int32, kbm.shape, 2)
    named = jnp.max(jnp.where(lane == me, kbm[...], -1.0), axis=2, keepdims=True)
    for j in range(n):
        hit = jnp.where((named == float(j)) | (me < GLOB), 0.0, -jnp.inf)
        bias[j] = jnp.broadcast_to(jnp.max(hit, axis=1, keepdims=True), (heads, 1, tokens))

    for t in range(1, nc):
        forward(0, t)

    def pair(g, t, peak):
        at = src_chip(t)
        if t == 0:
            own_k[g].wait()
            arrived(k_all.at[g, sib], k_snd.at[g, 0], k_rcv.at[g, 0])
        else:
            arrived(k_all.at[g, 2 * at + 1 - core], kf_snd.at[g, t], kf_rcv.at[g, t])
        x = k_all[g, pl.ds(2 * at, 2)].reshape(2 * tokens, hd).astype(F32)
        inv = lax.rsqrt(jnp.mean(x * x, axis=1, keepdims=True) + EPSILON)
        x = x * inv
        k_hat[t, g] = x
        x = x * k_gain
        k_tr[t, g] = x.T.astype(BF16)
        s = jnp.dot(x.astype(BF16), q_tr[g], preferred_element_type=F32)
        for i in range(2):
            line = jnp.concatenate([bias[2 * at + i, h] for h in range(g * per, (g + 1) * per)], axis=1)
            part = s[i * tokens:(i + 1) * tokens] + line
            s_scr[t, g, i * tokens:(i + 1) * tokens, :] = part
            peak = jnp.maximum(peak, jnp.max(part.reshape(tokens // 8, 8, wide), axis=0))
        if t == 0:
            own_v[g].wait()
            arrived(v_all.at[g, sib], v_snd.at[g, 0], v_rcv.at[g, 0])
        else:
            arrived(v_all.at[g, 2 * at + 1 - core], vf_snd.at[g, t], vf_rcv.at[g, t])
        vals = v_all[g, pl.ds(2 * at, 2)].reshape(2 * tokens, hd)
        p_scr[t, g] = jnp.dot(vals, d_tr[g], preferred_element_type=F32)
        return peak

    def hand_on(g, t):
        arrived(sib_in.at[g, t], s_snd.at[g, t], s_rcv.at[g, t])
        chip_out[g, t] = (acc[g, t, core] + sib_in[g, t].astype(F32)).astype(BF16)
        go(send(chip_out.at[g, t], chip_in.at[g, t], x_snd.at[g, t], x_rcv.at[g, t], seq=2 * src_chip(t) + core))

    k_part = jnp.zeros((1, hd), F32)
    order = list(range(1, nc)) + [0]
    waiting = []
    for g in range(groups):
        peak = jnp.full((8, wide), -jnp.inf, F32)
        for t in range(nc):
            peak = pair(g, t, peak)
            if t == 0:
                while waiting:
                    hand_on(*waiting.pop(0))
        if g + 1 < groups:
            for t in range(1, nc):
                forward(g + 1, t)
            query_tiles(g + 1)
        peak = jnp.max(peak, axis=0, keepdims=True)
        total = jnp.zeros((8, wide), F32)
        cross = jnp.zeros((8, wide), F32)
        for t in range(nc):
            for r in range(0, 2 * tokens, CHUNK):
                rows = slice(r, r + CHUNK)
                e = jnp.exp2((s_scr[t, g, rows, :] - peak) * raise_by)
                s_scr[t, g, rows, :] = e
                total = total + fold_rows(e)
                cross = cross + fold_rows(e * p_scr[t, g, rows, :])
        total = jnp.sum(total, axis=0, keepdims=True)
        cross = jnp.sum(cross, axis=0, keepdims=True)
        norm = 1.0 / total
        delta = cross * norm
        for t in order:
            for r in range(0, 2 * tokens, CHUNK):
                rows = slice(r, r + CHUNK)
                w = s_scr[t, g, rows, :] * norm
                w_scr[t, rows, :] = w.astype(BF16)
                ds_scr[t, g, rows, :] = (w * ((p_scr[t, g, rows, :] - delta) * scale)).astype(BF16)
            dk = jnp.dot(ds_scr[t, g], q_st[g], preferred_element_type=F32)
            dv = jnp.dot(w_scr[t], d_st[g], preferred_element_type=F32)
            for i in range(2):
                acc[g, t, i, 0] = dk[i * tokens:(i + 1) * tokens]
                acc[g, t, i, 1] = dv[i * tokens:(i + 1) * tokens]
            k_part = k_part + jnp.sum(dk * k_hat[t, g], axis=0, keepdims=True)
            sib_out[g, t] = acc[g, t, 1 - core].astype(BF16)
            go(send(sib_out.at[g, t], sib_in.at[g, t], s_snd.at[g, t], s_rcv.at[g, t], seq=sib))
            if waiting:
                hand_on(*waiting.pop(0))
            if t != 0:
                waiting.append((g, t))

    q_part = k_part * k_gain / q_gain
    part1[md] = jnp.concatenate([q_part, k_part, jnp.zeros((6, hd), F32)], axis=0)
    for r in range(1, dpn):
        go(send(part1.at[md], part1.at[md], p1_snd.at[r], p1_rcv.at[r], dp=lax.rem(md + r, dpn)))
    for g in range(groups):
        dq_tr = jnp.zeros((hd, wide), F32)
        for t in range(nc):
            dq_tr = dq_tr + jnp.dot(k_tr[t, g], ds_scr[t, g], preferred_element_type=F32)
        while waiting:
            hand_on(*waiting.pop(0))
        for i in range(per):
            h = g * per + i
            dq = dq_tr[:, i * tokens:(i + 1) * tokens].T.astype(BF16).astype(F32)
            x = q_hat[h]
            y = dq * q_gain
            mean = jnp.mean(y * x, axis=1, keepdims=True)
            q_out[:, h * hd:(h + 1) * hd] = (q_inv[h] * (y - x * mean)).astype(BF16)
        if g == 0:
            for r in range(1, dpn):
                arrived(part1.at[lax.rem(md + dpn - r, dpn)], p1_snd.at[r], p1_rcv.at[r])
            gains = part1[0]
            for i in range(1, dpn):
                gains = gains + part1[i]
            part2[me] = gains
            for r in range(1, n):
                go(send(part2.at[me], part2.at[me], p2_snd.at[r], p2_rcv.at[r], seq=lax.rem(me + r, n)))

    totals = []
    for g in range(groups):
        arrived(sib_in.at[g, 0], s_snd.at[g, 0], s_rcv.at[g, 0])
        totals.append(acc[g, 0, core] + sib_in[g, 0].astype(F32))
    for g in range(groups):
        total = totals[g]
        for t in range(1, nc):
            arrived(chip_in.at[g, t], x_snd.at[g, t], x_rcv.at[g, t])
            total = total + chip_in[g, t].astype(F32)
        cols = slice(g * hd, (g + 1) * hd)
        v_out[:, cols] = total[1].astype(BF16)
        x = k_all[g, me].astype(F32)
        inv = lax.rsqrt(jnp.mean(x * x, axis=1, keepdims=True) + EPSILON)
        x = x * inv
        y = total[0].astype(BF16).astype(F32) * k_gain
        mean = jnp.mean(y * x, axis=1, keepdims=True)
        k_out[:, cols] = (inv * (y - x * mean)).astype(BF16)

    for r in range(1, n):
        arrived(part2.at[lax.rem(me + n - r, n)], p2_snd.at[r], p2_rcv.at[r])
    gains = part2[0]
    for i in range(1, n):
        gains = gains + part2[i]
    share = hd // dpn
    mine = jnp.zeros((8, share), F32)
    for i in range(dpn):
        mine = mine + jnp.where(md == i, gains[:, i * share:(i + 1) * share], 0.0)
    gq_out[...] = mine[0:1]
    gk_out[...] = mine[1:2]

    for copy in pending:
        copy.wait_send()


def store_kernel(*refs):
    sems = refs[10]
    copies = [pltpu.make_async_copy(refs[i], refs[5 + i], sems.at[i]) for i in range(5)]
    for copy in copies:
        copy.start()
    for copy in copies:
        copy.wait()


def scratch_list(n, dpn, tokens, hd, heads, groups, held, blocks, slots):
    nc = n // 2
    wide = heads // groups * tokens
    vm = pltpu.VMEM
    dma = pltpu.SemaphoreType.DMA
    arrays = [
        vm((tokens, heads * hd), BF16),
        vm((tokens, heads * hd), BF16),
        vm((groups, n, tokens, hd), BF16),
        vm((groups, n, tokens, hd), BF16),
        vm((n, slots, held, blocks), jnp.int32),
        vm((heads, slots, blocks), F32),
        vm((dpn, 1, hd // dpn), F32),
        vm((dpn, 1, hd // dpn), F32),
        vm((n, heads, 1, tokens), F32),
        vm((heads, tokens, hd), F32),
        vm((heads, tokens, hd), F32),
        vm((groups, wide, hd), BF16),
        vm((groups, hd, wide), BF16),
        vm((groups, wide, hd), BF16),
        vm((groups, hd, wide), BF16),
        vm((nc, groups, 2 * tokens, hd), F32),
        vm((nc, groups, hd, 2 * tokens), BF16),
        vm((nc, groups, 2 * tokens, wide), F32),
        vm((nc, groups, 2 * tokens, wide), F32),
        vm((nc, groups, 2 * tokens, wide), BF16),
        vm((nc, 2 * tokens, wide), BF16),
        vm((groups, nc, 2, 2, tokens, hd), F32),
        vm((groups, nc, 2, tokens, hd), BF16),
        vm((groups, nc, 2, tokens, hd), BF16),
        vm((groups, nc, 2, tokens, hd), BF16),
        vm((groups, nc, 2, tokens, hd), BF16),
        vm((dpn, 8, hd), F32),
        vm((n, 8, hd), F32),
    ]
    sems = [dma((7 + 2 * groups,))] + [dma((groups, nc))] * 8 + [dma((n,))] * 2 + [dma((dpn,))] * 4
    sems += [dma((groups, nc))] * 4 + [dma((dpn,))] * 2 + [dma((n,))] * 2
    return arrays, sems


def shards(n, dpn, q_raw, k_raw, v_raw, q_gain, k_gain, key_blocks, d_context):
    hd = q_gain.shape[0] * dpn
    tokens = q_raw.shape[1]
    heads = q_raw.shape[2] // hd
    groups = k_raw.shape[2] // hd
    held, blocks, slots = key_blocks.shape
    arrays, sems = scratch_list(n, dpn, tokens, hd, heads, groups, held, blocks, slots)
    room = sum(math.prod(a.shape) * jnp.dtype(a.dtype).itemsize for a in arrays)
    fits = room < VMEM_ROOM - 16 * 1024 * 1024
    if n % 2 or tokens != BLK or q_raw.shape[0] != 1 or not fits:
        return shards_by_head(q_raw, k_raw, v_raw, q_gain, k_gain, key_blocks, d_context)
    anywhere = pl.BlockSpec(memory_space=pl.ANY)
    vmem = pl.BlockSpec(memory_space=pltpu.VMEM)
    share = hd // dpn
    kvd = groups * hd
    q_grad, k_grad, v_grad, gq, gk = pl.pallas_call(
        functools.partial(token_kernel, n, dpn),
        out_shape=(
            pltpu.VMEM((tokens, heads * hd), BF16),
            pltpu.VMEM((tokens, kvd), BF16),
            pltpu.VMEM((tokens, kvd), BF16),
            pltpu.VMEM((1, share), F32),
            pltpu.VMEM((1, share), F32),
        ),
        in_specs=[anywhere] * 7,
        out_specs=(vmem,) * 5,
        scratch_shapes=arrays + sems,
        compiler_params=pltpu.CompilerParams(
            collective_id=0, has_side_effects=True, vmem_limit_bytes=VMEM_ROOM
        ),
    )(q_raw[0], k_raw[0], v_raw[0], q_gain[None], k_gain[None], key_blocks.transpose(2, 0, 1), d_context[0])
    done = (q_grad, k_grad, v_grad, gq, gk)
    done = pl.pallas_call(
        store_kernel,
        out_shape=tuple(jax.ShapeDtypeStruct(x.shape, x.dtype) for x in done),
        in_specs=[vmem] * 5,
        out_specs=(anywhere,) * 5,
        scratch_shapes=[pltpu.SemaphoreType.DMA((5,))],
        compiler_params=pltpu.CompilerParams(vmem_limit_bytes=4 * 1024 * 1024),
    )(*done)
    return (done[0][None], done[1][None], done[2][None], done[3][0], done[4][0])


def solution(mesh):
    placed = (
        P("dp", "seq", None),
        P("dp", "seq", None),
        P("dp", "seq", None),
        P("dp"),
        P("dp"),
        P("seq", None, None),
        P("dp", "seq", None),
    )
    return jax.shard_map(
        functools.partial(shards, mesh.shape["seq"], mesh.shape["dp"]),
        mesh=mesh,
        in_specs=placed,
        out_specs=(
            P("dp", "seq", None),
            P("dp", "seq", None),
            P("dp", "seq", None),
            P("dp"),
            P("dp"),
        ),
        check_vma=False,
    )
```
